512 devices in a mesh: dp: 16 (over z), expert: 32 (over x, y, core).
Axes of the slice: x: 4, y: 4, z: 16, core: 2. Of those that a mesh axis runs over, the one named last changes fastest.
Arguments:
- cotangent: bfloat16 [65536, 1440], P(('dp', 'expert')), may hold values from -0.0625 to 0.0625
- gates: bfloat16 [65536, 4], P(('dp', 'expert')), may hold values from 0.049804688 to 0.59765625
- routes: int32 [65536, 4], P(('dp', 'expert')), may hold values from 0 to 31, as said below
- slots: int32 [65536, 4], P(('dp', 'expert')), may hold values from 0 to 31, as said below
- saved_hidden: bfloat16 [16, 32, 32, 32, 1440], P('dp', 'expert'), may hold values from -6 to 6
- left_wide: bfloat16 [32, 960, 960], P('expert', None, 'dp')
- left_narrow: bfloat16 [32, 480, 480], P('expert', None, 'dp')
- right_wide: bfloat16 [32, 960, 960], P('expert', None, 'dp')
- right_narrow: bfloat16 [32, 480, 480], P('expert', None, 'dp')
Outputs:
- precond_wide: float32 [32, 1440, 960], P('expert', None, 'dp')
- precond_narrow: float32 [32, 1440, 480], P('expert', None, 'dp')
The draws below stay inside these ranges and needn't reach their ends.
Inputs may be any that keep to these rules, and one draw needn't show every extreme that they name: Each row names 4 different experts. On each device the experts fall into groups of four and a token's routes name one whole group; no expert is named more than 32 times by the tokens of one device, and one expert is named exactly 32 times by the tokens of every device. slots[t, k] is the row of route k of token t in the buffer of 32 rows that its device fills for that expert; the routes of one device to one expert have different slots.
All inputs are finite; a program needn't handle non-finite values.
Results may differ from the reference program's by a relative error of at most 0.024.
Values may be sent and summed in bfloat16 or wider, within the bound.
A program may use at most 64 MiB of HBM per device.

```python
import math
import jax
import jax.numpy as jnp
from jax import lax

TOK_DEV = 128
TOPK = 4
FFN = 1440
DMODEL = 1440
BLOCK = 960
REM_F = 480
REM_D = 480
EXPERTS = 32
SOURCES = 32
CAP = 32
TOKENS = 65536
N_DP = 16


def device_routes(device_key, hot_expert):
    key_order, key_place, key_turn, key_slots = jax.random.split(device_key, 4)
    groups = EXPERTS // 4
    virtual_order = jax.random.permutation(key_order, EXPERTS).astype(jnp.int32)
    hot_place = jnp.argmax(virtual_order == hot_expert)
    leading = virtual_order[0]
    virtual_order = virtual_order.at[hot_place].set(leading).at[0].set(hot_expert)
    full_class = min(CAP, TOK_DEV)
    remaining = TOK_DEV - full_class
    class_index = jnp.arange(groups, dtype=jnp.int32)
    others = remaining // (groups - 1) + (class_index - 1 < remaining % (groups - 1)).astype(jnp.int32)
    class_size = jnp.where(class_index == 0, full_class, others).astype(jnp.int32)
    class_end = jnp.cumsum(class_size)
    class_start = class_end - class_size
    placement = jax.random.permutation(key_place, TOK_DEV).astype(jnp.int32)
    token_class = jnp.sum((placement[:, None] >= class_end[None, :]).astype(jnp.int32), axis=1)
    class_rank = placement - class_start[token_class]
    rotation = jax.random.randint(key_turn, (TOK_DEV,), 0, 4)
    route_index = jnp.arange(4, dtype=jnp.int32)
    virtual = token_class[:, None] + groups * ((rotation[:, None] + route_index[None, :]) % 4)
    routes_here = virtual_order[virtual]

    def slot_order(slot_key):
        return jax.random.permutation(slot_key, CAP).astype(jnp.int32)
    slot_tables = jax.vmap(slot_order)(jax.random.split(key_slots, EXPERTS))
    slots_here = slot_tables[virtual, class_rank[:, None]]
    return (routes_here.astype(jnp.int32), slots_here.astype(jnp.int32))


def route_table(key):
    key_hot, key_device = jax.random.split(key)
    hot_expert = jax.random.randint(key_hot, (), 0, EXPERTS).astype(jnp.int32)
    device_keys = jax.random.split(key_device, TOKENS // TOK_DEV)
    routes_all, slots_all = jax.vmap(device_routes, in_axes=(0, None))(device_keys, hot_expert)
    return (routes_all.reshape(TOKENS, 4), slots_all.reshape(TOKENS, 4))


def symmetric_root(key, count, size, off_scale, diag_low):
    key_off, key_diag = jax.random.split(key)
    normals = jnp.clip(jax.random.normal(key_off, (count, size, size), jnp.float32), -4.0, 4.0)
    mirrored = (normals + jnp.swapaxes(normals, 1, 2)) * (off_scale / math.sqrt(2.0 * size))
    identity = jnp.eye(size, dtype=jnp.float32)
    diagonal = jax.random.uniform(key_diag, (count, size, 1), jnp.float32, diag_low, 2.0)
    return (mirrored * (1.0 - identity) + identity * diagonal).astype(jnp.bfloat16)


def draw_routes(key, part):
    table = route_table(key)
    return table[0]


def draw_slots(key, part):
    table = route_table(key)
    return table[1]


def draw_left_wide(key, part):
    key = jax.random.fold_in(key, 11)
    return symmetric_root(key, EXPERTS, BLOCK, 0.4, 1.0)


def draw_left_narrow(key, part):
    key = jax.random.fold_in(key, 12)
    return symmetric_root(key, EXPERTS, REM_F, 0.4, 1.0)


def draw_right_wide(key, part):
    key = jax.random.fold_in(key, 13)
    return symmetric_root(key, EXPERTS, BLOCK, 0.4, 1.0)


def draw_right_narrow(key, part):
    key = jax.random.fold_in(key, 14)
    return symmetric_root(key, EXPERTS, REM_D, 0.4, 1.0)


def levels(rng, dims, cuts, least, largest):
    def one(position, blocks):
        steps = jax.random.uniform(jax.random.fold_in(jax.random.fold_in(rng, 6), position), (blocks,), jnp.float32, least / len(cuts), largest / len(cuts))
        return jnp.repeat(jnp.exp(steps), dims[position] // blocks).reshape((-1,) + (1,) * (len(dims) - position - 1))

    factor_of = one(*cuts[0])
    for cut in cuts[1:]:
        factor_of = factor_of * one(*cut)
    return factor_of


def bell_draw(stream_key, dims, deviation, most, shards=(), kind=jnp.bfloat16):
    result = deviation * jax.random.normal(stream_key, dims, jnp.float32)
    if shards:
        result = result * levels(stream_key, dims, shards, -0.22, 0.18)
    return jnp.clip(result, -most, most).astype(kind)


def setup_inputs(seed: int = 0) -> dict:
    arg_keys = jax.random.split(jax.random.key(seed), 10)
    cotangent = bell_draw(arg_keys[0], (TOKENS, DMODEL), 0.01, 0.0625, ((0, 512),))
    gates = jnp.clip(0.049804688 + 0.54785156 * jax.random.uniform(arg_keys[1], (TOKENS, TOPK), jnp.float32) ** levels(arg_keys[1], (TOKENS, TOPK), ((0, 512),), -0.2, 0.2), 0.049804688, 0.59765625).astype(jnp.bfloat16)
    routes = draw_routes(jax.random.fold_in(arg_keys[9], 71), 0)
    slots = draw_slots(jax.random.fold_in(arg_keys[9], 71), 0)
    saved_hidden = bell_draw(arg_keys[4], (N_DP, EXPERTS, SOURCES, CAP, FFN), 1.0, 6.0, ((0, 16), (1, 32)))
    left_wide = draw_left_wide(jax.random.fold_in(arg_keys[9], 71), 0)
    left_narrow = draw_left_narrow(jax.random.fold_in(arg_keys[9], 71), 0)
    right_wide = draw_right_wide(jax.random.fold_in(arg_keys[9], 71), 0)
    right_narrow = draw_right_narrow(jax.random.fold_in(arg_keys[9], 71), 0)
    return dict(cotangent=cotangent, gates=gates, routes=routes, slots=slots, saved_hidden=saved_hidden, left_wide=left_wide, left_narrow=left_narrow, right_wide=right_wide, right_narrow=right_narrow)


def row_partial(cotangent_rows, gate_rows, route_rows, slot_rows, hidden_rows):
    scaled_rows = (gate_rows.astype(jnp.float32)[:, :, None] * cotangent_rows.astype(jnp.float32)[:, None, :]).astype(jnp.bfloat16)
    source_index = (jnp.arange(cotangent_rows.shape[0], dtype=jnp.int32) // TOK_DEV)[:, None]
    target = ((route_rows * SOURCES + source_index) * CAP + slot_rows).reshape(-1)
    buffer = jnp.zeros((EXPERTS * SOURCES * CAP, DMODEL), jnp.bfloat16).at[target].set(scaled_rows.reshape(-1, DMODEL))
    buffer = buffer.reshape(EXPERTS, SOURCES * CAP, DMODEL).astype(jnp.float32)
    hidden = hidden_rows.reshape(EXPERTS, SOURCES * CAP, FFN).astype(jnp.float32)
    partial_value = jnp.einsum("erh,erd->ehd", hidden, buffer)
    return partial_value.astype(jnp.bfloat16)


def reference(cotangent, gates, routes, slots, saved_hidden, left_wide, left_narrow, right_wide, right_narrow):
    row_tokens = TOK_DEV * SOURCES
    cotangent_rows = cotangent.reshape(N_DP, row_tokens, DMODEL)
    gate_rows = gates.reshape(N_DP, row_tokens, TOPK)
    route_rows = routes.reshape(N_DP, row_tokens, TOPK)
    slot_rows = slots.reshape(N_DP, row_tokens, TOPK)

    def accumulate(running, pieces):
        partial_value = lax.optimization_barrier(row_partial(*pieces))
        return running + partial_value.astype(jnp.float32), None

    gradient, _ = lax.scan(accumulate, jnp.zeros((EXPERTS, FFN, DMODEL), jnp.float32),
                           (cotangent_rows, gate_rows, route_rows, slot_rows, saved_hidden))
    gradient_bf = lax.optimization_barrier(gradient.astype(jnp.bfloat16)).astype(jnp.float32)
    precise = lax.Precision.HIGHEST
    right_product = jnp.concatenate([
        jnp.einsum("ehb,ebc->ehc", gradient_bf[:, :, :BLOCK], right_wide.astype(jnp.float32), precision=precise),
        jnp.einsum("ehb,ebc->ehc", gradient_bf[:, :, BLOCK:], right_narrow.astype(jnp.float32), precision=precise)], axis=2)
    right_bf = lax.optimization_barrier(right_product.astype(jnp.bfloat16)).astype(jnp.float32)
    stacked = jnp.concatenate([
        jnp.einsum("eab,ebd->ead", left_wide.astype(jnp.float32), right_bf[:, :BLOCK, :], precision=precise),
        jnp.einsum("eab,ebd->ead", left_narrow.astype(jnp.float32), right_bf[:, BLOCK:, :], precision=precise)], axis=1)
    return stacked[:, :, :BLOCK], stacked[:, :, BLOCK:]
```

```python
import functools

import jax
import jax.numpy as jnp
from jax import lax
from jax.experimental import pallas as pl
from jax.experimental.pallas import tpu as pltpu
from jax.sharding import PartitionSpec as P

MESH = pl.DeviceIdType.MESH
BF = jnp.bfloat16
F32 = jnp.float32
LANE = 128


def up(value, unit):
    return -(-value // unit) * unit


def nn(left, right):
    return lax.dot_general(left, right, (((1,), (0,)), ((), ())), preferred_element_type=F32)


def nt(left, right):
    return lax.dot_general(left, right, (((1,), (1,)), ((), ())), preferred_element_type=F32)


class Sizes:
    def __init__(self, ring, experts, capacity, width, wide, narrow, tokens, routes):
        self.ring, self.experts, self.capacity = ring, experts, capacity
        self.width, self.wide, self.narrow = width, wide, narrow
        self.tokens, self.routes = tokens, routes
        self.wp, self.np = up(wide, LANE), up(narrow, LANE)
        self.full = self.wp + self.np
        self.cw, self.cn = wide // ring, narrow // ring
        self.cwp, self.cnp = up(self.cw, 32), up(self.cn, 32)
        self.seg = self.cwp + self.cnp
        self.half = ring // 2
        self.rows = experts * capacity
        self.kchunks = min(4, experts)
        self.kblocks = experts // self.kchunks
        self.krows = self.kblocks * capacity
        self.tile = min(256, self.np)


def kernel(
    z, cot_ref, gates_ref, routes_ref, slots_ref, hid_hbm, lw_ref, ln_ref, rw_ref, rn_ref,
    ow_ref, on_ref,
    hid_v, at, cotp, outb, inb, acc, part, rtw, rtn, ltw, ltn, ht, land, lwc, lnc,
    hid_sem, a2a_send, a2a_recv, ag_send, ag_recv, rs_send, rs_recv,
):
    n, half, experts = z.ring, z.half, z.experts
    zi = lax.axis_index("dp")
    ei = lax.axis_index("expert")
    plus = (lax.rem(zi + 1, n), ei)
    minus = (lax.rem(zi + n - 1, n), ei)
    neighbour = (plus, minus)

    barrier = pltpu.get_barrier_semaphore()
    for target in neighbour:
        pl.semaphore_signal(barrier, inc=1, device_id=target, device_id_type=MESH)

    def greet(k, carry):
        pl.semaphore_signal(
            barrier, inc=1, device_id=(zi, lax.rem(ei + k, experts)), device_id_type=MESH
        )
        return carry

    lax.fori_loop(1, experts, greet, 0)

    def hidden_copy(k):
        return pltpu.make_async_copy(
            hid_hbm.at[lax.rem(ei + k, experts)], hid_v.at[k], hid_sem.at[k]
        )

    def hidden_start(k, carry):
        hidden_copy(k).start()
        return carry

    lax.fori_loop(0, experts, hidden_start, 0)

    for dst, src, rows, cols in (
        (rtw, rw_ref, z.cw, z.wide), (rtn, rn_ref, z.cn, z.narrow),
        (ltw, lw_ref, z.cw, z.wide), (ltn, ln_ref, z.cn, z.narrow),
    ):
        dst[0] = jnp.zeros(dst.shape[1:], BF)
        dst[0, :rows, :cols] = src[...]

    cotp[...] = jnp.zeros_like(cotp)
    cotp[: z.wide, :] = cot_ref[: z.wide, :]
    cotp[z.wp : z.wp + z.narrow, :] = cot_ref[z.wide :, :]
    place = routes_ref[...] * z.capacity + slots_ref[...]
    gate = gates_ref[...].astype(F32)

    def build(block, carry):
        row = lax.broadcasted_iota(jnp.int32, (z.krows, z.tokens), 0) + block * z.krows
        weight = jnp.zeros((z.krows, z.tokens), F32)
        for k in range(z.routes):
            weight = weight + jnp.where(row == place[k : k + 1, :], gate[k : k + 1, :], 0.0)
        rows = nt(weight.astype(BF), cotp[...]).astype(BF)
        outb[pl.ds(block * z.kblocks, z.kblocks)] = rows.reshape(z.kblocks, z.capacity, z.full)
        return carry

    lax.fori_loop(0, z.kchunks, build, 0)

    pl.semaphore_wait(barrier, experts + 1)

    def gather_copies(kind, direction, step):
        copies = []
        for piece, buf in enumerate(((rtw, rtn), (ltw, ltn))[kind]):
            if direction == 0:
                src, dst = (n - step + 1) % n, n - step
            else:
                src, dst = step - 1, step
            src_ref, dst_ref = buf.at[src], buf.at[dst]
            if step == half:
                middle = buf.shape[1] // 2
                rows = pl.ds(direction * middle, middle)
                src_ref, dst_ref = buf.at[src, rows], buf.at[dst, rows]
            copies.append(pltpu.make_async_remote_copy(
                src_ref=src_ref, dst_ref=dst_ref,
                send_sem=ag_send.at[kind, direction, step - 1, piece],
                recv_sem=ag_recv.at[kind, direction, step - 1, piece],
                device_id=neighbour[direction], device_id_type=MESH,
            ))
        return copies

    def gather_start(kind, step):
        for direction in range(2):
            for copy in gather_copies(kind, direction, step):
                copy.start()

    def gather_step(kind, step):
        for direction in range(2):
            for copy in gather_copies(kind, direction, step):
                copy.wait_recv()
            if step < half:
                for copy in gather_copies(kind, direction, step + 1):
                    copy.start()

    gather_start(0, 1)

    def routed_copy(k):
        partner = lax.rem(ei + experts - k, experts)
        return pltpu.make_async_remote_copy(
            src_ref=outb.at[partner], dst_ref=inb.at[k],
            send_sem=a2a_send.at[k], recv_sem=a2a_recv.at[k],
            device_id=(zi, partner), device_id_type=MESH,
        )

    def routed_start(k, carry):
        routed_copy(k).start()
        return carry

    lax.fori_loop(1, experts, routed_start, 0)
    gather_start(1, 1)
    inb[0] = outb[ei]

    def hidden_wait(k, carry):
        hidden_copy(k).wait()
        return carry

    lax.fori_loop(0, experts, hidden_wait, 0)

    at[z.wide : z.wp, :] = jnp.zeros((z.wp - z.wide, z.rows), BF)
    at[z.wp + z.narrow :, :] = jnp.zeros((z.np - z.narrow, z.rows), BF)
    for first in range(0, z.width, LANE):
        size = min(LANE, z.width - first)
        turned = hid_v[:, :, first : first + size].reshape(z.rows, size).T
        cut = min(max(z.wide - first, 0), size)
        if cut > 0:
            at[first : first + cut, :] = turned[:cut]
        if cut < size:
            base = first + cut - z.wide + z.wp
            at[base : base + size - cut, :] = turned[cut:]

    def accumulate(chunk):
        def arrived(k, carry):
            routed_copy(k).wait_recv()
            return carry

        lax.fori_loop(max(chunk * z.kblocks, 1), (chunk + 1) * z.kblocks, arrived, 0)

        def tile(m, carry):
            rows = pl.ds(pl.multiple_of(m * z.tile, z.tile), z.tile)
            piece = inb[chunk * z.kblocks : (chunk + 1) * z.kblocks].reshape(z.krows, z.full)
            value = nn(at[rows, chunk * z.krows : (chunk + 1) * z.krows], piece)
            if chunk > 0:
                value = value + acc[rows, :]
            if chunk < z.kchunks - 1:
                acc[rows, :] = value
            else:
                part[rows, :] = value.astype(BF)
            return carry

        lax.fori_loop(0, z.full // z.tile, tile, 0)

    def right(first, count):
        def tile(m, carry):
            cols = pl.ds(pl.multiple_of(m * z.tile, z.tile), z.tile)
            wide = nt(rtw[first : first + count].reshape(count * z.cwp, z.wp), part[cols, : z.wp])
            narrow = nt(rtn[first : first + count].reshape(count * z.cnp, z.np), part[cols, z.wp :])
            ht[first : first + count, : z.cwp, cols] = wide.astype(BF).reshape(count, z.cwp, z.tile)
            ht[first : first + count, z.cwp :, cols] = narrow.astype(BF).reshape(count, z.cnp, z.tile)
            return carry

        lax.fori_loop(0, z.full // z.tile, tile, 0)

    late = {half - 3 + c: c for c in range(z.kchunks)} if half >= 8 else {}
    for step in range(1, half + 1):
        gather_step(0, step)
        gather_step(1, step)
        if step in late:
            accumulate(late[step])
    for chunk in range(z.kchunks):
        if chunk not in late.values():
            accumulate(chunk)

    middle = z.seg // 2

    def hops(direction, piece):
        return half if direction == piece else half - 1

    def own_slot(direction, distance):
        return distance if direction == 0 else (n - distance) % n

    def reduce_copy(direction, piece, hop):
        rows = pl.ds(piece * middle, middle)
        if hop == 1:
            src = ht.at[own_slot(direction, hops(direction, piece)), rows]
        else:
            src = land.at[direction, hop - 2, rows]
        return pltpu.make_async_remote_copy(
            src_ref=src, dst_ref=land.at[direction, hop - 1, rows],
            send_sem=rs_send.at[direction, piece, hop - 1],
            recv_sem=rs_recv.at[direction, piece, hop - 1],
            device_id=neighbour[direction], device_id_type=MESH,
        )

    group = max(1, n // 4)
    start = half - group // 2
    right(start, group)
    lanes = ((0, 0), (1, 1), (0, 1), (1, 0))
    for direction, piece in lanes:
        reduce_copy(direction, piece, 1).start()
    right(start + group, group)
    right(start - group, group)

    def reduce_step(hop):
        for direction, piece in lanes:
            if hop >= hops(direction, piece):
                continue
            reduce_copy(direction, piece, hop).wait_recv()
            rows = slice(piece * middle, (piece + 1) * middle)
            slot = own_slot(direction, hops(direction, piece) - hop)
            total = land[direction, hop - 1, rows].astype(F32) + ht[slot, rows].astype(F32)
            land[direction, hop - 1, rows] = total.astype(BF)
            reduce_copy(direction, piece, hop + 1).start()

    def compact(dst, src, count, unit, valid):
        shift = unit.bit_length() - 1
        depth = n * unit

        def tile(m, carry):
            rows = pl.ds(pl.multiple_of(m * z.tile, z.tile), z.tile)
            feature = lax.broadcasted_iota(jnp.int32, (z.tile, depth), 0) + m * z.tile
            place = lax.broadcasted_iota(jnp.int32, (z.tile, depth), 1)
            owner = (zi + lax.shift_right_logical(place, shift)) & (n - 1)
            inner = place & (unit - 1)
            pick = jnp.where((feature == owner * valid + inner) & (inner < valid), 1.0, 0.0)
            dst[rows, :] = nn(pick.astype(BF), src[...].reshape(depth, src.shape[2])).astype(BF)
            return carry

        lax.fori_loop(0, count // z.tile, tile, 0)

    for hop in range(1, half):
        reduce_step(hop)
        if hop == 1:
            if start + 2 * group < n:
                right(start + 2 * group, n - start - 2 * group)
            if start - group > 0:
                right(0, start - group)
            compact(lwc, ltw, z.wp, z.cwp, z.cw)
            compact(lnc, ltn, z.np, z.cnp, z.cn)

    sums = []
    for piece in range(2):
        rows = slice(piece * middle, (piece + 1) * middle)
        total = ht[0, rows].astype(F32)
        for direction in range(2):
            hop = hops(direction, piece)
            reduce_copy(direction, piece, hop).wait_recv()
            total = total + land[direction, hop - 1, rows].astype(F32)
        sums.append(total.astype(BF))
    final = jnp.concatenate(sums, axis=0)
    upper = nn(final[:, : z.wp], lwc[...])
    lower = nn(final[:, z.wp :], lnc[...])
    ow_ref[:, : z.wide] = upper[: z.cw, : z.wide]
    ow_ref[:, z.wide :] = lower[: z.cw, : z.narrow]
    on_ref[:, : z.wide] = upper[z.cwp : z.cwp + z.cn, : z.wide]
    on_ref[:, z.wide :] = lower[z.cwp : z.cwp + z.cn, : z.narrow]

    def routed_sent(k, carry):
        routed_copy(k).wait_send()
        return carry

    lax.fori_loop(1, experts, routed_sent, 0)
    for kind in range(2):
        for step in range(1, half + 1):
            for direction in range(2):
                for copy in gather_copies(kind, direction, step):
                    copy.wait_send()
    for direction, piece in lanes:
        for hop in range(1, hops(direction, piece) + 1):
            reduce_copy(direction, piece, hop).wait_send()


def body(
    cotangent, gates, routes, slots, saved_hidden, left_wide, left_narrow, right_wide, right_narrow
):
    ring, experts = lax.axis_size("dp"), lax.axis_size("expert")
    capacity, width = saved_hidden.shape[3:]
    z = Sizes(
        ring, experts, capacity, width, left_wide.shape[1], left_narrow.shape[1],
        cotangent.shape[0], gates.shape[1],
    )
    vmem = pl.BlockSpec(memory_space=pltpu.VMEM)
    ow, on = pl.pallas_call(
        functools.partial(kernel, z),
        out_shape=(
            jax.ShapeDtypeStruct((z.cw, z.width), F32),
            jax.ShapeDtypeStruct((z.cn, z.width), F32),
        ),
        in_specs=[vmem] * 4 + [pl.BlockSpec(memory_space=pl.ANY)] + [vmem] * 4,
        out_specs=(vmem, vmem),
        scratch_shapes=[
            pltpu.VMEM((experts, capacity, width), BF),
            pltpu.VMEM((z.full, z.rows), BF),
            pltpu.VMEM((z.full, z.tokens), BF),
            pltpu.VMEM((experts, capacity, z.full), BF),
            pltpu.VMEM((experts, capacity, z.full), BF),
            pltpu.VMEM((z.full, z.full), F32),
            pltpu.VMEM((z.full, z.full), BF),
            pltpu.VMEM((ring, z.cwp, z.wp), BF),
            pltpu.VMEM((ring, z.cnp, z.np), BF),
            pltpu.VMEM((ring, z.cwp, z.wp), BF),
            pltpu.VMEM((ring, z.cnp, z.np), BF),
            pltpu.VMEM((ring, z.seg, z.full), BF),
            pltpu.VMEM((2, z.half, z.seg, z.full), BF),
            pltpu.VMEM((z.wp, z.wp), BF),
            pltpu.VMEM((z.np, z.np), BF),
            pltpu.SemaphoreType.DMA((experts,)),
            pltpu.SemaphoreType.DMA((experts,)),
            pltpu.SemaphoreType.DMA((experts,)),
            pltpu.SemaphoreType.DMA((2, 2, z.half, 2)),
            pltpu.SemaphoreType.DMA((2, 2, z.half, 2)),
            pltpu.SemaphoreType.DMA((2, 2, z.half)),
            pltpu.SemaphoreType.DMA((2, 2, z.half)),
        ],
        compiler_params=pltpu.CompilerParams(
            collective_id=0, has_side_effects=True, vmem_limit_bytes=60 * 1024 * 1024
        ),
        cost_estimate=pl.CostEstimate(flops=10_000_000_000, bytes_accessed=8_000_000, transcendentals=0),
    )(
        cotangent.T, gates.T, routes.T, slots.T,
        saved_hidden.reshape(experts, capacity, width),
        left_wide[0].T, left_narrow[0].T, right_wide[0].T, right_narrow[0].T,
    )
    return ow.T[None], on.T[None]


def solution(mesh):
    return jax.shard_map(
        body,
        mesh=mesh,
        in_specs=(
            P(("dp", "expert"), None),
            P(("dp", "expert"), None),
            P(("dp", "expert"), None),
            P(("dp", "expert"), None),
            P("dp", "expert", None, None, None),
            P("expert", None, "dp"),
            P("expert", None, "dp"),
            P("expert", None, "dp"),
            P("expert", None, "dp"),
        ),
        out_specs=(P("expert", None, "dp"), P("expert", None, "dp")),
        check_vma=False,
    )
```

```python
import functools
import math

import jax
import jax.numpy as jnp
from jax import lax
from jax.experimental import pallas as pl
from jax.experimental.pallas import tpu as pltpu
from jax.sharding import PartitionSpec as P

MESH = pl.DeviceIdType.MESH
BF = jnp.bfloat16
F32 = jnp.float32
LANE = 128


def up(value, unit):
    return -(-value // unit) * unit


def nn(left, right):
    return lax.dot_general(left, right, (((1,), (0,)), ((), ())), preferred_element_type=F32)


def nt(left, right):
    return lax.dot_general(left, right, (((1,), (1,)), ((), ())), preferred_element_type=F32)


class Sizes:
    def __init__(self, ring, experts, capacity, width, wide, narrow, tokens, routes):
        self.ring, self.experts, self.capacity = ring, experts, capacity
        self.width, self.wide, self.narrow = width, wide, narrow
        self.tokens, self.routes = tokens, routes
        self.cw, self.cn = wide // ring, narrow // ring
        self.cwp, self.cnp = up(self.cw, 32), up(self.cn, 32)
        self.seg = self.cwp + self.cnp
        self.half = ring // 2
        self.side = math.isqrt(experts // 2)
        self.part = width // 2
        self.meta = up(3 * routes, 16)
        self.rows = self.meta + self.part
        self.sources = 2 * self.side
        self.depth = self.sources * capacity
        self.mtile = self.part // 3
        self.pick = narrow // 2


def kernel(
    z, cot_ref, gates_ref, routes_ref, slots_ref, hid_hbm, lw_ref, ln_ref, rw_ref, rn_ref,
    ow_ref, on_ref,
    hid_v, cg, wt, acc, part, rtw, rtn, ltw, ltn, ht, land, lwc, lnc,
    hid_sem, p_send, p_recv, q_send, q_recv, s_send, s_recv, ag_send, ag_recv, rs_send, rs_recv,
):
    n, half, side = z.ring, z.half, z.side
    zi = lax.axis_index("dp")
    ei = lax.axis_index("expert")
    core = lax.rem(ei, 2)
    yi = lax.rem(ei // 2, side)
    xi = ei // (2 * side)

    def expert_at(x, y, c):
        return (x * side + y) * 2 + c

    def step_to(index, direction):
        return lax.rem(index + (1 if direction == 0 else side - 1), side)

    ring_to = ((lax.rem(zi + 1, n), ei), (lax.rem(zi + n - 1, n), ei))
    x_to = tuple((zi, expert_at(step_to(xi, d), yi, core)) for d in range(2))
    y_to = tuple((zi, expert_at(xi, step_to(yi, d), core)) for d in range(2))
    sibling = (zi, expert_at(xi, yi, 1 - core))
    axis_to = (x_to, y_to)

    barrier = pltpu.get_barrier_semaphore()
    for target in (*ring_to, *x_to, *y_to, sibling):
        pl.semaphore_signal(barrier, inc=1, device_id=target, device_id_type=MESH)

    def hidden_copy(k):
        dx, dy, dc = k // (2 * side), lax.rem(k // 2, side), lax.rem(k, 2)
        source = expert_at(
            lax.rem(xi + dx, side), lax.rem(yi + dy, side), lax.rem(core + dc, 2)
        )
        return pltpu.make_async_copy(hid_hbm.at[source], hid_v.at[dx, dy, dc], hid_sem.at[k])

    def hidden_start(k, carry):
        hidden_copy(k).start()
        return carry

    lax.fori_loop(0, z.experts, hidden_start, 0)

    for dst, src, rows in (
        (rtw, rw_ref, z.cw), (rtn, rn_ref, z.cn), (ltw, lw_ref, z.cw), (ltn, ln_ref, z.cn)
    ):
        dst[0] = jnp.zeros(dst.shape[1:], BF)
        dst[0, :rows] = src[...]
    spare = jnp.zeros((z.meta - 3 * z.routes, z.tokens), F32)
    meta = jnp.concatenate(
        [gates_ref[...].astype(F32), routes_ref[...].astype(F32), slots_ref[...].astype(F32), spare],
        axis=0,
    ).astype(BF)
    for h in range(2):
        cg[h, 0, 0, 0, : z.meta] = meta
        cg[h, 0, 0, 0, z.meta :] = cot_ref[h * z.part : (h + 1) * z.part]
    wt[...] = jnp.zeros_like(wt)

    pl.semaphore_wait(barrier, 7)

    def gather_copies(kind, direction, step):
        copies = []
        for piece, buf in enumerate(((rtw, rtn), (ltw, ltn))[kind]):
            if direction == 0:
                src, dst = (n - step + 1) % n, n - step
            else:
                src, dst = step - 1, step
            src_ref, dst_ref = buf.at[src], buf.at[dst]
            if step == half:
                middle = buf.shape[1] // 2
                rows = pl.ds(direction * middle, middle)
                src_ref, dst_ref = buf.at[src, rows], buf.at[dst, rows]
            copies.append(pltpu.make_async_remote_copy(
                src_ref=src_ref, dst_ref=dst_ref,
                send_sem=ag_send.at[kind, direction, step - 1, piece],
                recv_sem=ag_recv.at[kind, direction, step - 1, piece],
                device_id=ring_to[direction], device_id_type=MESH,
            ))
        return copies

    def gather_start(kind, step):
        for direction in range(2):
            for copy in gather_copies(kind, direction, step):
                copy.start()

    def gather_step(kind, step):
        for direction in range(2):
            for copy in gather_copies(kind, direction, step):
                copy.wait_recv()
            if step < half:
                for copy in gather_copies(kind, direction, step + 1):
                    copy.start()

    def came_from(direction):
        return side - 1 if direction == 0 else 1

    def share(direction):
        return pl.ds(direction * (z.rows // 2), z.rows // 2)

    def first_copy(h, stage, direction):
        if stage == 0:
            src, dst = cg.at[h, 0, 0, 0], cg.at[h, came_from(direction), 0, 0]
        else:
            src = cg.at[h, came_from(direction), 0, 0, share(direction)]
            dst = cg.at[h, 2, 0, 0, share(direction)]
        return pltpu.make_async_remote_copy(
            src_ref=src, dst_ref=dst,
            send_sem=p_send.at[h, stage, direction], recv_sem=p_recv.at[h, stage, direction],
            device_id=axis_to[h][direction], device_id_type=MESH,
        )

    def second_copy(h, stage, i, direction):
        if stage == 0:
            src, dst = cg.at[h, i, 0, 0], cg.at[h, i, came_from(direction), 0]
        else:
            src = cg.at[h, i, came_from(direction), 0, share(direction)]
            dst = cg.at[h, i, 2, 0, share(direction)]
        return pltpu.make_async_remote_copy(
            src_ref=src, dst_ref=dst,
            send_sem=q_send.at[h, stage, i, direction], recv_sem=q_recv.at[h, stage, i, direction],
            device_id=axis_to[1 - h][direction], device_id_type=MESH,
        )

    def sibling_copy(h, i, j):
        return pltpu.make_async_remote_copy(
            src_ref=cg.at[h, i, j, 0], dst_ref=cg.at[h, i, j, 1],
            send_sem=s_send.at[h, i, j], recv_sem=s_recv.at[h, i, j],
            device_id=sibling, device_id_type=MESH,
        )

    both = tuple((h, d) for d in range(2) for h in range(2))

    def first_arrived():
        for h, d in both:
            first_copy(h, 0, d).wait_recv()
            first_copy(h, 1, d).start()
            i = came_from(d)
            for e in range(2):
                second_copy(h, 0, i, e).start()
            sibling_copy(h, i, 0).start()

    def first_far_arrived():
        for h in range(2):
            for d in range(2):
                first_copy(h, 1, d).wait_recv()
            for e in range(2):
                second_copy(h, 0, 2, e).start()
            sibling_copy(h, 2, 0).start()

    def second_arrived(i):
        for h, d in both:
            second_copy(h, 0, i, d).wait_recv()
            second_copy(h, 1, i, d).start()
            sibling_copy(h, i, came_from(d)).start()

    def second_far_arrived(i):
        for h in range(2):
            for d in range(2):
                second_copy(h, 1, i, d).wait_recv()
            sibling_copy(h, i, 2).start()

    gather_start(0, 1)
    for h, d in both:
        first_copy(h, 0, d).start()
    for h, d in both:
        second_copy(h, 0, 0, d).start()
    gather_start(1, 1)
    for h in range(2):
        sibling_copy(h, 0, 0).start()

    def hidden_wait(k, carry):
        hidden_copy(k).wait()
        return carry

    lax.fori_loop(0, z.experts, hidden_wait, 0)

    def accumulate(h, j, is_first, is_last):
        for i in range(side):
            sibling_copy(h, i, j).wait_recv()
        place = lax.broadcasted_iota(jnp.int32, (z.capacity, z.tokens), 0).astype(F32)
        mine = ei.astype(F32)
        for s in range(z.sources):
            info = cg[h, s // 2, j, s % 2, : z.meta].astype(F32)
            weight = jnp.zeros((z.capacity, z.tokens), F32)
            for k in range(z.routes):
                gate = info[k : k + 1]
                route = info[z.routes + k : z.routes + k + 1]
                slot = info[2 * z.routes + k : 2 * z.routes + k + 1]
                weight = weight + jnp.where((route == mine) & (slot == place), gate, 0.0)
            wt[
                s * z.capacity : (s + 1) * z.capacity, s * z.tokens : (s + 1) * z.tokens
            ] = weight.astype(BF)

        def tile(m, carry):
            inner = pl.ds(pl.multiple_of(z.meta + m * z.mtile, 16), z.mtile)
            rows = pl.ds(pl.multiple_of(h * z.part + m * z.mtile, 16), z.mtile)
            left = jnp.concatenate(
                [cg[h, s // 2, j, s % 2, inner, :] for s in range(z.sources)], axis=1
            )
            routed = nt(left, wt[...]).astype(BF)
            hidden = hid_v[:, j] if h == 0 else hid_v[j]
            value = nn(routed, hidden.reshape(z.depth, z.width))
            if not is_first:
                value = value + acc[rows, :]
            if is_last:
                part[rows, :] = value.astype(BF)
            else:
                acc[rows, :] = value
            return carry

        lax.fori_loop(0, z.part // z.mtile, tile, 0)

    def right(first, count):
        for base in range(0, z.width, 512):
            cols = slice(base, min(base + 512, z.width))
            size = cols.stop - cols.start
            wide = nn(rtw[first : first + count].reshape(count * z.cwp, z.wide), part[: z.wide, cols])
            narrow = nn(rtn[first : first + count].reshape(count * z.cnp, z.narrow), part[z.wide :, cols])
            ht[first : first + count, : z.cwp, cols] = wide.astype(BF).reshape(count, z.cwp, size)
            ht[first : first + count, z.cwp :, cols] = narrow.astype(BF).reshape(count, z.cnp, size)

    def chunk(j, is_first=False, is_last=False):
        for h in range(2):
            accumulate(h, j, is_first, is_last)

    plan = [
        (first_arrived,), (0, 1), (1, 1), (second_arrived, 0), (0, 2), (first_far_arrived,),
        (chunk, 0, True), (1, 2), (second_arrived, side - 1), (second_arrived, 1), (0, 3), (1, 3),
        (second_arrived, 2), (0, 4), (chunk, 1), (chunk, side - 1), (1, 4),
        (second_far_arrived, 0), (second_far_arrived, side - 1), (second_far_arrived, 1),
        (0, 5), (second_far_arrived, 2), (1, 5), (chunk, 2, False, True),
    ]
    ringed = []
    for entry in plan:
        if callable(entry[0]):
            entry[0](*entry[1:])
        elif entry[1] <= half:
            gather_step(*entry)
            ringed.append(entry)
    for step in range(1, half + 1):
        for kind in range(2):
            if (kind, step) not in ringed and (kind, step) != (1, half):
                gather_step(kind, step)

    middle = z.seg // 2

    def hops(direction, piece):
        return half if direction == piece else half - 1

    def own_slot(direction, distance):
        return distance if direction == 0 else (n - distance) % n

    def reduce_copy(direction, piece, hop):
        rows = pl.ds(piece * middle, middle)
        if hop == 1:
            src = ht.at[own_slot(direction, hops(direction, piece)), rows]
        else:
            src = land.at[direction, hop - 2, rows]
        return pltpu.make_async_remote_copy(
            src_ref=src, dst_ref=land.at[direction, hop - 1, rows],
            send_sem=rs_send.at[direction, piece, hop - 1],
            recv_sem=rs_recv.at[direction, piece, hop - 1],
            device_id=ring_to[direction], device_id_type=MESH,
        )

    lanes = ((0, 0), (1, 1), (0, 1), (1, 0))
    small = n < 16
    group = n // 4
    start = half - group // 2
    if small:
        right(0, n)
    else:
        right(start, group)
    for direction, piece in lanes:
        if hops(direction, piece) > 0:
            reduce_copy(direction, piece, 1).start()
    if not small:
        right(start + group, group)
        right(start - group, group)

    def reduce_step(hop):
        for direction, piece in lanes:
            if hop >= hops(direction, piece):
                continue
            reduce_copy(direction, piece, hop).wait_recv()
            rows = slice(piece * middle, (piece + 1) * middle)
            slot = own_slot(direction, hops(direction, piece) - hop)
            total = land[direction, hop - 1, rows].astype(F32) + ht[slot, rows].astype(F32)
            land[direction, hop - 1, rows] = total.astype(BF)
            reduce_copy(direction, piece, hop + 1).start()

    def compact(dst, src, count, unit, valid):
        shift = unit.bit_length() - 1
        depth = n * unit

        def tile(m, carry):
            rows = pl.ds(pl.multiple_of(m * z.pick, 16), z.pick)
            feature = lax.broadcasted_iota(jnp.int32, (z.pick, depth), 0) + m * z.pick
            place = lax.broadcasted_iota(jnp.int32, (z.pick, depth), 1)
            owner = (zi + lax.shift_right_logical(place, shift)) & (n - 1)
            inner = place & (unit - 1)
            pick = jnp.where((feature == owner * valid + inner) & (inner < valid), 1.0, 0.0)
            dst[rows, :] = nn(pick.astype(BF), src[...].reshape(depth, src.shape[2])).astype(BF)
            return carry

        lax.fori_loop(0, count // z.pick, tile, 0)

    def compact_left():
        gather_step(1, half)
        compact(lwc, ltw, z.wide, z.cwp, z.cw)
        compact(lnc, ltn, z.narrow, z.cnp, z.cn)

    for hop in range(1, half):
        reduce_step(hop)
        if hop == 1 and not small:
            right(start + 2 * group, n - start - 2 * group)
            right(0, start - group)
        if hop == min(3, half - 1):
            compact_left()
    if half == 1:
        compact_left()

    sums = []
    for piece in range(2):
        rows = slice(piece * middle, (piece + 1) * middle)
        total = ht[0, rows].astype(F32)
        for direction in range(2):
            hop = hops(direction, piece)
            if hop > 0:
                reduce_copy(direction, piece, hop).wait_recv()
                total = total + land[direction, hop - 1, rows].astype(F32)
        sums.append(total.astype(BF))
    final = jnp.concatenate(sums, axis=0)
    upper = nn(final[:, : z.wide], lwc[...])
    lower = nn(final[:, z.wide :], lnc[...])
    ow_ref[:, : z.wide] = upper[: z.cw]
    ow_ref[:, z.wide :] = lower[: z.cw]
    on_ref[:, : z.wide] = upper[z.cwp : z.cwp + z.cn]
    on_ref[:, z.wide :] = lower[z.cwp : z.cwp + z.cn]

    for h in range(2):
        for d in range(2):
            for stage in range(2):
                first_copy(h, stage, d).wait_send()
                for i in range(side):
                    second_copy(h, stage, i, d).wait_send()
        for i in range(side):
            for j in range(side):
                sibling_copy(h, i, j).wait_send()
    for kind in range(2):
        for step in range(1, half + 1):
            for direction in range(2):
                for copy in gather_copies(kind, direction, step):
                    copy.wait_send()
    for direction, piece in lanes:
        for hop in range(1, hops(direction, piece) + 1):
            reduce_copy(direction, piece, hop).wait_send()


def body(
    cotangent, gates, routes, slots, saved_hidden, left_wide, left_narrow, right_wide, right_narrow
):
    ring, experts = lax.axis_size("dp"), lax.axis_size("expert")
    capacity, width = saved_hidden.shape[3:]
    z = Sizes(
        ring, experts, capacity, width, left_wide.shape[1], left_narrow.shape[1],
        cotangent.shape[0], gates.shape[1],
    )
    vmem = pl.BlockSpec(memory_space=pltpu.VMEM)
    ow, on = pl.pallas_call(
        functools.partial(kernel, z),
        out_shape=(
            jax.ShapeDtypeStruct((z.cw, z.width), F32),
            jax.ShapeDtypeStruct((z.cn, z.width), F32),
        ),
        in_specs=[vmem] * 4 + [pl.BlockSpec(memory_space=pl.ANY)] + [vmem] * 4,
        out_specs=(vmem, vmem),
        scratch_shapes=[
            pltpu.VMEM((z.side, z.side, 2, capacity, width), BF),
            pltpu.VMEM((2, z.side, z.side, 2, z.rows, z.tokens), BF),
            pltpu.VMEM((z.depth, z.sources * z.tokens), BF),
            pltpu.VMEM((width, width), F32),
            pltpu.VMEM((width, width), BF),
            pltpu.VMEM((ring, z.cwp, z.wide), BF),
            pltpu.VMEM((ring, z.cnp, z.narrow), BF),
            pltpu.VMEM((ring, z.cwp, z.wide), BF),
            pltpu.VMEM((ring, z.cnp, z.narrow), BF),
            pltpu.VMEM((ring, z.seg, width), BF),
            pltpu.VMEM((2, z.half, z.seg, width), BF),
            pltpu.VMEM((z.wide, z.wide), BF),
            pltpu.VMEM((z.narrow, z.narrow), BF),
            pltpu.SemaphoreType.DMA((experts,)),
            pltpu.SemaphoreType.DMA((2, 2, 2)),
            pltpu.SemaphoreType.DMA((2, 2, 2)),
            pltpu.SemaphoreType.DMA((2, 2, z.side, 2)),
            pltpu.SemaphoreType.DMA((2, 2, z.side, 2)),
            pltpu.SemaphoreType.DMA((2, z.side, z.side)),
            pltpu.SemaphoreType.DMA((2, z.side, z.side)),
            pltpu.SemaphoreType.DMA((2, 2, z.half, 2)),
            pltpu.SemaphoreType.DMA((2, 2, z.half, 2)),
            pltpu.SemaphoreType.DMA((2, 2, z.half)),
            pltpu.SemaphoreType.DMA((2, 2, z.half)),
        ],
        compiler_params=pltpu.CompilerParams(
            collective_id=0, has_side_effects=True, vmem_limit_bytes=60 * 1024 * 1024
        ),
        cost_estimate=pl.CostEstimate(flops=10_000_000_000, bytes_accessed=8_000_000, transcendentals=0),
    )(
        cotangent.T, gates.T, routes.T, slots.T,
        saved_hidden.reshape(experts, capacity, width),
        left_wide[0].T, left_narrow[0].T, right_wide[0].T, right_narrow[0].T,
    )
    return ow.T[None], on.T[None]


def solution(mesh):
    return jax.shard_map(
        body,
        mesh=mesh,
        in_specs=(
            P(("dp", "expert"), None),
            P(("dp", "expert"), None),
            P(("dp", "expert"), None),
            P(("dp", "expert"), None),
            P("dp", "expert", None, None, None),
            P("expert", None, "dp"),
            P("expert", None, "dp"),
            P("expert", None, "dp"),
            P("expert", None, "dp"),
        ),
        out_specs=(P("expert", None, "dp"), P("expert", None, "dp")),
        check_vma=False,
    )
```

```python
import functools
import math

import jax
import jax.numpy as jnp
from jax import lax
from jax.experimental import pallas as pl
from jax.experimental.pallas import tpu as pltpu
from jax.sharding import PartitionSpec as P

MESH = pl.DeviceIdType.MESH
BF = jnp.bfloat16
F32 = jnp.float32
LANE = 128


def up(value, unit):
    return -(-value // unit) * unit


def nn(left, right):
    return lax.dot_general(left, right, (((1,), (0,)), ((), ())), preferred_element_type=F32)


def nt(left, right):
    return lax.dot_general(left, right, (((1,), (1,)), ((), ())), preferred_element_type=F32)


class Sizes:
    def __init__(self, ring, experts, capacity, width, wide, narrow, tokens, routes):
        self.ring, self.experts, self.capacity = ring, experts, capacity
        self.width, self.wide, self.narrow = width, wide, narrow
        self.tokens, self.routes = tokens, routes
        self.cw, self.cn = wide // ring, narrow // ring
        self.cwp, self.cnp = up(self.cw, 32), up(self.cn, 32)
        self.seg = self.cwp + self.cnp
        self.half = ring // 2
        self.side = math.isqrt(experts // 2)
        self.part = width // 2
        self.meta = up(3 * routes, 16)
        self.rows = self.meta + self.part
        self.sources = 2 * self.side
        self.depth = self.sources * capacity
        self.rest = width % LANE
        self.kept = width - self.rest
        self.tiles = ((0, 512), (512, 1024), (1024, width))
        self.pick = narrow // 2


def kernel(
    z, cot_ref, gates_ref, routes_ref, slots_ref, hid_hbm, lw_ref, ln_ref, rw_ref, rn_ref,
    ow_ref, on_ref,
    hid_v, cg, wt, bt, acc, part, rtw, rtn, ltw, ltn, ht, land, lwc, lnc,
    hid_sem, p_send, p_recv, q_send, q_recv, s_send, s_recv, ag_send, ag_recv, rs_send, rs_recv,
):
    n, half, side = z.ring, z.half, z.side
    zi = lax.axis_index("dp")
    ei = lax.axis_index("expert")
    core = lax.rem(ei, 2)
    yi = lax.rem(ei // 2, side)
    xi = ei // (2 * side)

    def expert_at(x, y, c):
        return (x * side + y) * 2 + c

    def step_to(index, direction):
        return lax.rem(index + (1 if direction == 0 else side - 1), side)

    ring_to = ((lax.rem(zi + 1, n), ei), (lax.rem(zi + n - 1, n), ei))
    x_to = tuple((zi, expert_at(step_to(xi, d), yi, core)) for d in range(2))
    y_to = tuple((zi, expert_at(xi, step_to(yi, d), core)) for d in range(2))
    sibling = (zi, expert_at(xi, yi, 1 - core))
    axis_to = (x_to, y_to)

    barrier = pltpu.get_barrier_semaphore()
    for target in (*ring_to, *x_to, *y_to, sibling):
        pl.semaphore_signal(barrier, inc=1, device_id=target, device_id_type=MESH)

    def hidden_copy(k):
        dx, dy, dc = k // (2 * side), lax.rem(k // 2, side), lax.rem(k, 2)
        source = expert_at(
            lax.rem(xi + dx, side), lax.rem(yi + dy, side), lax.rem(core + dc, 2)
        )
        return pltpu.make_async_copy(hid_hbm.at[source], hid_v.at[dx, dy, dc], hid_sem.at[k])

    def hidden_start(k, carry):
        hidden_copy(k).start()
        return carry

    lax.fori_loop(0, z.experts, hidden_start, 0)

    for dst, src, rows in (
        (rtw, rw_ref, z.cw), (rtn, rn_ref, z.cn), (ltw, lw_ref, z.cw), (ltn, ln_ref, z.cn)
    ):
        dst[0] = jnp.zeros(dst.shape[1:], BF)
        dst[0, :rows] = src[...]
    spare = jnp.zeros((z.meta - 3 * z.routes, z.tokens), F32)
    meta = jnp.concatenate(
        [gates_ref[...].astype(F32), routes_ref[...].astype(F32), slots_ref[...].astype(F32), spare],
        axis=0,
    ).astype(BF)
    for h in range(2):
        cg[h, 0, 0, 0, : z.meta] = meta
        cg[h, 0, 0, 0, z.meta :] = cot_ref[h * z.part : (h + 1) * z.part]
    wt[...] = jnp.zeros_like(wt)

    pl.semaphore_wait(barrier, 7)

    def gather_copies(kind, direction, step):
        copies = []
        for piece, buf in enumerate(((rtw, rtn), (ltw, ltn))[kind]):
            if direction == 0:
                src, dst = (n - step + 1) % n, n - step
            else:
                src, dst = step - 1, step
            src_ref, dst_ref = buf.at[src], buf.at[dst]
            if step == half:
                middle = buf.shape[1] // 2
                rows = pl.ds(direction * middle, middle)
                src_ref, dst_ref = buf.at[src, rows], buf.at[dst, rows]
            copies.append(pltpu.make_async_remote_copy(
                src_ref=src_ref, dst_ref=dst_ref,
                send_sem=ag_send.at[kind, direction, step - 1, piece],
                recv_sem=ag_recv.at[kind, direction, step - 1, piece],
                device_id=ring_to[direction], device_id_type=MESH,
            ))
        return copies

    def gather_start(kind, step):
        for direction in range(2):
            for copy in gather_copies(kind, direction, step):
                copy.start()

    def gather_step(kind, step):
        for direction in range(2):
            for copy in gather_copies(kind, direction, step):
                copy.wait_recv()
            if step < half:
                for copy in gather_copies(kind, direction, step + 1):
                    copy.start()

    def came_from(direction):
        return side - 1 if direction == 0 else 1

    def share(direction):
        return pl.ds(direction * (z.rows // 2), z.rows // 2)

    def first_copy(h, stage, direction):
        if stage == 0:
            src, dst = cg.at[h, 0, 0, 0], cg.at[h, came_from(direction), 0, 0]
        else:
            src = cg.at[h, came_from(direction), 0, 0, share(direction)]
            dst = cg.at[h, 2, 0, 0, share(direction)]
        return pltpu.make_async_remote_copy(
            src_ref=src, dst_ref=dst,
            send_sem=p_send.at[h, stage, direction], recv_sem=p_recv.at[h, stage, direction],
            device_id=axis_to[h][direction], device_id_type=MESH,
        )

    def second_copy(h, stage, i, direction):
        if stage == 0:
            src, dst = cg.at[h, i, 0, 0], cg.at[h, i, came_from(direction), 0]
        else:
            src = cg.at[h, i, came_from(direction), 0, share(direction)]
            dst = cg.at[h, i, 2, 0, share(direction)]
        return pltpu.make_async_remote_copy(
            src_ref=src, dst_ref=dst,
            send_sem=q_send.at[h, stage, i, direction], recv_sem=q_recv.at[h, stage, i, direction],
            device_id=axis_to[1 - h][direction], device_id_type=MESH,
        )

    def sibling_copy(h, i, j):
        return pltpu.make_async_remote_copy(
            src_ref=cg.at[h, i, j, 0], dst_ref=cg.at[h, i, j, 1],
            send_sem=s_send.at[h, i, j], recv_sem=s_recv.at[h, i, j],
            device_id=sibling, device_id_type=MESH,
        )

    both = tuple((h, d) for d in range(2) for h in range(2))

    def first_arrived():
        for h, d in both:
            first_copy(h, 0, d).wait_recv()
            first_copy(h, 1, d).start()
            i = came_from(d)
            for e in range(2):
                second_copy(h, 0, i, e).start()
            sibling_copy(h, i, 0).start()

    def first_far_arrived():
        for h in range(2):
            for d in range(2):
                first_copy(h, 1, d).wait_recv()
            for e in range(2):
                second_copy(h, 0, 2, e).start()
            sibling_copy(h, 2, 0).start()

    def second_arrived(i):
        for h, d in both:
            second_copy(h, 0, i, d).wait_recv()
            second_copy(h, 1, i, d).start()
            sibling_copy(h, i, came_from(d)).start()

    def second_far_arrived(i):
        for h in range(2):
            for d in range(2):
                second_copy(h, 1, i, d).wait_recv()
            sibling_copy(h, i, 2).start()

    gather_start(0, 1)
    for h, d in both:
        first_copy(h, 0, d).start()
    for h, d in both:
        second_copy(h, 0, 0, d).start()
    gather_start(1, 1)
    for h in range(2):
        sibling_copy(h, 0, 0).start()

    def hidden_wait(k, carry):
        hidden_copy(k).wait()
        return carry

    lax.fori_loop(0, z.experts, hidden_wait, 0)

    def prepare(h, j, place):
        for i in range(side):
            sibling_copy(h, i, j).wait_recv()
        slot_row = lax.broadcasted_iota(jnp.int32, (z.capacity, z.tokens), 0).astype(F32)
        mine = ei.astype(F32)
        for s in range(z.sources):
            info = cg[h, s // 2, j, s % 2, : z.meta].astype(F32)
            weight = jnp.zeros((z.capacity, z.tokens), F32)
            for k in range(z.routes):
                gate = info[k : k + 1]
                route = info[z.routes + k : z.routes + k + 1]
                slot = info[2 * z.routes + k : 2 * z.routes + k + 1]
                weight = weight + jnp.where((route == mine) & (slot == slot_row), gate, 0.0)
            wt[
                s * z.capacity : (s + 1) * z.capacity, s * z.tokens : (s + 1) * z.tokens
            ] = weight.astype(BF)
        left = jnp.concatenate(
            [cg[h, s // 2, j, s % 2, z.meta :, :] for s in range(z.sources)], axis=1
        )
        bt[:, place * z.depth : (place + 1) * z.depth] = nt(left, wt[...]).astype(BF)

    def add_tile(h, offsets, tile, is_first, is_last):
        cols = slice(*z.tiles[tile])
        rows = slice(h * z.part, (h + 1) * z.part)
        size = cols.stop - cols.start
        hidden = jnp.concatenate(
            [(hid_v[:, j, :, :, cols] if h == 0 else hid_v[j, :, :, :, cols]).reshape(z.depth, size)
             for j in offsets], axis=0,
        )
        value = nn(bt[:, : len(offsets) * z.depth], hidden)
        if not is_first:
            value = value + acc[rows, cols]
        if is_last:
            part[rows, cols] = value.astype(BF)
        else:
            acc[rows, cols] = value

    def right(first, count):
        for buf, unit, valid, lower, rows in (
            (rtw, z.cwp, z.cw, slice(0, z.wide), slice(0, z.cwp)),
            (rtn, z.cnp, z.cn, slice(z.wide, z.width), slice(z.cwp, z.seg)),
        ):
            left = buf[first : first + count].reshape(count * unit, buf.shape[2])
            tail = nn(left, part[lower, slice(*z.tiles[2])]).astype(BF)
            keep = z.kept - z.tiles[2][0]
            ht[first : first + count, rows, z.tiles[2][0] : z.kept] = tail[:, :keep].reshape(
                count, unit, keep
            )
            folded = fold(tail[:, keep:], count * unit, unit, valid)
            for tile in range(2):
                cols = slice(*z.tiles[tile])
                value = nn(left, part[lower, cols])
                if tile == 0:
                    value = value + folded
                ht[first : first + count, rows, cols] = value.astype(BF).reshape(
                    count, unit, cols.stop - cols.start
                )

    def spread(size):
        lane = lax.broadcasted_iota(jnp.int32, (z.rest, size), 1)
        return (lane & (z.rest - 1)) == lax.broadcasted_iota(jnp.int32, (z.rest, size), 0)

    def one(mask):
        return jnp.where(mask, 1.0, 0.0).astype(BF)

    def fold(rest, count, unit, valid):
        size = z.tiles[0][1]
        spare = unit - valid
        low = spare.bit_length() - 1
        shift = z.rest.bit_length() - 1
        wide = nn(rest, one(spread(size)))
        row = lax.broadcasted_iota(jnp.int32, (count, size), 0)
        lane = lax.broadcasted_iota(jnp.int32, (count, size), 1)
        own = lax.shift_right_logical(row & (unit - 1), low) == lax.shift_right_logical(lane, shift)
        wide = jnp.where(own, wide, 0.0).astype(BF)
        to = lax.broadcasted_iota(jnp.int32, (count, count), 0)
        frm = lax.broadcasted_iota(jnp.int32, (count, count), 1)
        same = (to & -unit) == (frm & -unit)
        pick = same & ((to & (unit - 1)) - valid == (frm & (spare - 1)))
        return nn(one(pick), wide)

    def unfold(final):
        size = z.tiles[0][1]
        shift = z.rest.bit_length() - 1
        spare_w, spare_n = z.cwp - z.cw, z.cnp - z.cn
        low_w, low_n = spare_w.bit_length() - 1, spare_n.bit_length() - 1
        to = lax.broadcasted_iota(jnp.int32, (z.seg, z.seg), 0)
        frm = lax.broadcasted_iota(jnp.int32, (z.seg, z.seg), 1)
        source = jnp.where(
            to < z.cwp, z.cw + (to & (spare_w - 1)), z.cwp + z.cn + (to & (spare_n - 1))
        )
        rows = nn(one(frm == source), final[:, :size])
        row = lax.broadcasted_iota(jnp.int32, (z.seg, size), 0)
        lane = lax.broadcasted_iota(jnp.int32, (z.seg, size), 1)
        place = jnp.where(
            row < z.cwp,
            lax.shift_right_logical(row, low_w),
            lax.shift_right_logical(row - z.cwp, low_n),
        )
        rows = jnp.where(place == lax.shift_right_logical(lane, shift), rows, 0.0).astype(BF)
        return nt(rows, one(spread(size))).astype(BF)

    middle = z.seg // 2

    def hops(direction, piece):
        return half if direction == piece else half - 1

    def own_slot(direction, distance):
        return distance if direction == 0 else (n - distance) % n

    def reduce_copy(direction, piece, hop):
        rows = pl.ds(piece * middle, middle)
        if hop == 1:
            src = ht.at[own_slot(direction, hops(direction, piece)), rows]
        else:
            src = land.at[direction, hop - 2, rows]
        return pltpu.make_async_remote_copy(
            src_ref=src, dst_ref=land.at[direction, hop - 1, rows],
            send_sem=rs_send.at[direction, piece, hop - 1],
            recv_sem=rs_recv.at[direction, piece, hop - 1],
            device_id=ring_to[direction], device_id_type=MESH,
        )

    lanes = ((0, 1), (1, 0), (0, 0), (1, 1))

    def reduce_step(hop):
        for direction, piece in lanes:
            if hop >= hops(direction, piece):
                continue
            reduce_copy(direction, piece, hop).wait_recv()
            rows = slice(piece * middle, (piece + 1) * middle)
            slot = own_slot(direction, hops(direction, piece) - hop)
            total = land[direction, hop - 1, rows].astype(F32) + ht[slot, rows].astype(F32)
            land[direction, hop - 1, rows] = total.astype(BF)
            reduce_copy(direction, piece, hop + 1).start()

    def compact(dst, src, unit, valid, m):
        shift = unit.bit_length() - 1
        depth = n * unit
        rows = slice(m * z.pick, (m + 1) * z.pick)
        feature = lax.broadcasted_iota(jnp.int32, (z.pick, depth), 0) + m * z.pick
        place = lax.broadcasted_iota(jnp.int32, (z.pick, depth), 1)
        owner = (zi + lax.shift_right_logical(place, shift)) & (n - 1)
        inner = place & (unit - 1)
        pick = one((feature == owner * valid + inner) & (inner < valid))
        dst[rows, :] = nn(pick, src[...].reshape(depth, src.shape[2])).astype(BF)

    def work(h, offsets, is_first=False, is_last=False):
        for place, j in enumerate(offsets):
            prepare(h, j, place)
            yield
        for tile in range(3):
            add_tile(h, offsets, tile, is_first, is_last)
            yield

    def run(*steps):
        for entry in steps:
            if isinstance(entry, int):
                for _ in range(entry):
                    next(jobs, None)
            else:
                entry[0](*entry[1:])

    def all_work():
        for h in range(2):
            yield from work(h, (0,), is_first=True)
        for h in range(2):
            yield from work(h, (1, side - 1))
        for h in range(2):
            yield from work(h, (2,), is_last=True)

    jobs = all_work()
    far = side - 1
    ring = gather_step
    run(
        (ring, 0, 1), (first_arrived,), (ring, 1, 1), (second_arrived, 0), (ring, 0, 2),
        (first_far_arrived,), 1, (ring, 1, 2), 3, (second_arrived, far), (ring, 0, 3), 3,
        (ring, 1, 3), 1, (second_arrived, 1), (ring, 0, 4), (second_arrived, 2), (ring, 1, 4),
        (second_far_arrived, 0), 2, (ring, 0, 5), (second_far_arrived, far), 3, (ring, 1, 5),
        (second_far_arrived, 1), 2, (ring, 0, 6), (second_far_arrived, 2), 3, (ring, 1, 6), 4,
        (ring, 0, 7), 4,
    )
    right(0, half)
    reduce_copy(0, 1, 1).start()
    gather_step(1, half - 1)
    right(half + 1, n - half - 1)
    reduce_copy(1, 0, 1).start()
    gather_step(0, half)
    right(half, 1)
    reduce_copy(0, 0, 1).start()
    reduce_copy(1, 1, 1).start()
    gather_step(1, half)

    later = [(lwc, ltw, z.cwp, z.cw, m) for m in range(z.wide // z.pick)]
    later += [(lnc, ltn, z.cnp, z.cn, m) for m in range(z.narrow // z.pick)]
    for hop in range(1, half):
        reduce_step(hop)
        if hop >= 2 and later:
            compact(*later.pop(0))
    for entry in later:
        compact(*entry)

    sums = []
    for piece in range(2):
        rows = slice(piece * middle, (piece + 1) * middle)
        total = ht[0, rows].astype(F32)
        for direction in range(2):
            hop = hops(direction, piece)
            if hop > 0:
                reduce_copy(direction, piece, hop).wait_recv()
                total = total + land[direction, hop - 1, rows].astype(F32)
        sums.append(total.astype(BF))
    final = jnp.concatenate(sums, axis=0)
    upper = nn(final[:, : z.wide], lwc[...])
    lower = nn(final[:, z.wide :], lnc[: z.kept - z.wide]) + nn(unfold(final), lnc[z.kept - z.wide :])
    result = jnp.concatenate([upper, lower], axis=1)
    ow_ref[:, 0, :] = result[: z.cw]
    on_ref[:, 0, :] = result[z.cwp : z.cwp + z.cn]

    for h in range(2):
        for d in range(2):
            for stage in range(2):
                first_copy(h, stage, d).wait_send()
                for i in range(side):
                    second_copy(h, stage, i, d).wait_send()
        for i in range(side):
            for j in range(side):
                sibling_copy(h, i, j).wait_send()
    for kind in range(2):
        for step in range(1, half + 1):
            for direction in range(2):
                for copy in gather_copies(kind, direction, step):
                    copy.wait_send()
    for direction, piece in lanes:
        for hop in range(1, hops(direction, piece) + 1):
            reduce_copy(direction, piece, hop).wait_send()


def body(
    cotangent, gates, routes, slots, saved_hidden, left_wide, left_narrow, right_wide, right_narrow
):
    ring, experts = lax.axis_size("dp"), lax.axis_size("expert")
    capacity, width = saved_hidden.shape[3:]
    z = Sizes(
        ring, experts, capacity, width, left_wide.shape[1], left_narrow.shape[1],
        cotangent.shape[0], gates.shape[1],
    )
    vmem = pl.BlockSpec(memory_space=pltpu.VMEM)
    ow, on = pl.pallas_call(
        functools.partial(kernel, z),
        out_shape=(
            jax.ShapeDtypeStruct((z.cw, 1, z.width), F32),
            jax.ShapeDtypeStruct((z.cn, 1, z.width), F32),
        ),
        in_specs=[vmem] * 4 + [pl.BlockSpec(memory_space=pl.ANY)] + [vmem] * 4,
        out_specs=(vmem, vmem),
        scratch_shapes=[
            pltpu.VMEM((z.side, z.side, 2, capacity, width), BF),
            pltpu.VMEM((2, z.side, z.side, 2, z.rows, z.tokens), BF),
            pltpu.VMEM((z.depth, z.sources * z.tokens), BF),
            pltpu.VMEM((z.part, 2 * z.depth), BF),
            pltpu.VMEM((width, width), F32),
            pltpu.VMEM((width, width), BF),
            pltpu.VMEM((ring, z.cwp, z.wide), BF),
            pltpu.VMEM((ring, z.cnp, z.narrow), BF),
            pltpu.VMEM((ring, z.cwp, z.wide), BF),
            pltpu.VMEM((ring, z.cnp, z.narrow), BF),
            pltpu.VMEM((ring, z.seg, z.kept), BF),
            pltpu.VMEM((2, z.half, z.seg, z.kept), BF),
            pltpu.VMEM((z.wide, z.wide), BF),
            pltpu.VMEM((z.narrow, z.narrow), BF),
            pltpu.SemaphoreType.DMA((experts,)),
            pltpu.SemaphoreType.DMA((2, 2, 2)),
            pltpu.SemaphoreType.DMA((2, 2, 2)),
            pltpu.SemaphoreType.DMA((2, 2, z.side, 2)),
            pltpu.SemaphoreType.DMA((2, 2, z.side, 2)),
            pltpu.SemaphoreType.DMA((2, z.side, z.side)),
            pltpu.SemaphoreType.DMA((2, z.side, z.side)),
            pltpu.SemaphoreType.DMA((2, 2, z.half, 2)),
            pltpu.SemaphoreType.DMA((2, 2, z.half, 2)),
            pltpu.SemaphoreType.DMA((2, 2, z.half)),
            pltpu.SemaphoreType.DMA((2, 2, z.half)),
        ],
        compiler_params=pltpu.CompilerParams(
            collective_id=0, has_side_effects=True, vmem_limit_bytes=60 * 1024 * 1024
        ),
        cost_estimate=pl.CostEstimate(flops=10_000_000_000, bytes_accessed=8_000_000, transcendentals=0),
    )(
        cotangent.T, gates.T, routes.T, slots.T,
        saved_hidden.reshape(experts, capacity, width),
        left_wide[0].T, left_narrow[0].T, right_wide[0].T, right_narrow[0].T,
    )
    return jnp.transpose(ow, (1, 2, 0)), jnp.transpose(on, (1, 2, 0))


def solution(mesh):
    return jax.shard_map(
        body,
        mesh=mesh,
        in_specs=(
            P(("dp", "expert"), None),
            P(("dp", "expert"), None),
            P(("dp", "expert"), None),
            P(("dp", "expert"), None),
            P("dp", "expert", None, None, None),
            P("expert", None, "dp"),
            P("expert", None, "dp"),
            P("expert", None, "dp"),
            P("expert", None, "dp"),
        ),
        out_specs=(P("expert", None, "dp"), P("expert", None, "dp")),
        check_vma=False,
    )
```

```python
import functools
import math

import jax
import jax.numpy as jnp
from jax import lax
from jax.experimental import pallas as pl
from jax.experimental.pallas import tpu as pltpu
from jax.sharding import PartitionSpec as P

MESH = pl.DeviceIdType.MESH
BF = jnp.bfloat16
F32 = jnp.float32
LANE = 128


def up(value, unit):
    return -(-value // unit) * unit


def nn(left, right):
    return lax.dot_general(left, right, (((1,), (0,)), ((), ())), preferred_element_type=F32)


def nt(left, right):
    return lax.dot_general(left, right, (((1,), (1,)), ((), ())), preferred_element_type=F32)


class Sizes:
    def __init__(self, ring, experts, capacity, width, wide, narrow, tokens, routes):
        self.ring, self.experts, self.capacity = ring, experts, capacity
        self.width, self.wide, self.narrow = width, wide, narrow
        self.tokens, self.routes = tokens, routes
        self.cw, self.cn = wide // ring, narrow // ring
        self.cwp, self.cnp = up(self.cw, 32), up(self.cn, 32)
        self.seg = self.cwp + self.cnp
        self.half = ring // 2
        self.side = math.isqrt(experts // 2)
        self.part = width // 2
        self.meta = up(3 * routes, 16)
        self.rows = self.meta + self.part
        self.sources = 2 * self.side
        self.depth = self.sources * capacity
        self.rest = width % LANE
        self.kept = width - self.rest
        self.tiles = ((0, 512), (512, 1024), (1024, width))
        self.pick = narrow // 2
        self.beside = 2 * narrow // 5
        self.tail = narrow - 2 * self.beside
        self.packed = wide + self.beside
        self.spare = self.cwp - self.cw
        self.folds = self.cnp // self.spare
        self.folded = self.folds * self.tail


def kernel(
    z, cot_ref, gates_ref, routes_ref, slots_ref, hid_hbm, lw_ref, ln_ref, rw_ref, rn_ref,
    ow_ref, on_ref,
    hid_v, cg, wt, bt, acc, part, rtp, rtn, ltp, ltn, spr, ht, land, lwc, lnc,
    hid_sem, p_send, p_recv, q_send, q_recv, s_send, s_recv, ag_send, ag_recv, rs_send, rs_recv,
):
    n, half, side = z.ring, z.half, z.side
    zi = lax.axis_index("dp")
    ei = lax.axis_index("expert")
    core = lax.rem(ei, 2)
    yi = lax.rem(ei // 2, side)
    xi = ei // (2 * side)

    def expert_at(x, y, c):
        return (x * side + y) * 2 + c

    def step_to(index, direction):
        return lax.rem(index + (1 if direction == 0 else side - 1), side)

    ring_to = ((lax.rem(zi + 1, n), ei), (lax.rem(zi + n - 1, n), ei))
    x_to = tuple((zi, expert_at(step_to(xi, d), yi, core)) for d in range(2))
    y_to = tuple((zi, expert_at(xi, step_to(yi, d), core)) for d in range(2))
    sibling = (zi, expert_at(xi, yi, 1 - core))
    axis_to = (x_to, y_to)

    barrier = pltpu.get_barrier_semaphore()
    for target in (*ring_to, *x_to, *y_to, sibling):
        pl.semaphore_signal(barrier, inc=1, device_id=target, device_id_type=MESH)

    def one(mask):
        return jnp.where(mask, 1.0, 0.0).astype(BF)

    def in_fold(count):
        row = lax.broadcasted_iota(jnp.int32, (count, z.folded), 0) & (z.cnp - 1)
        lane = lax.broadcasted_iota(jnp.int32, (count, z.folded), 1)
        low = lax.shift_right_logical(row, z.spare.bit_length() - 1) * z.tail
        return (lane >= low) & (lane < low + z.tail)

    def hidden_copy(k):
        dx, dy, dc = k // (2 * side), lax.rem(k // 2, side), lax.rem(k, 2)
        source = expert_at(
            lax.rem(xi + dx, side), lax.rem(yi + dy, side), lax.rem(core + dc, 2)
        )
        return pltpu.make_async_copy(hid_hbm.at[source], hid_v.at[dx, dy, dc], hid_sem.at[k])

    def hidden_start(k, carry):
        hidden_copy(k).start()
        return carry

    lax.fori_loop(0, z.experts, hidden_start, 0)

    lane = lax.broadcasted_iota(jnp.int32, (z.tail, z.folded), 1)
    base = lax.broadcasted_iota(jnp.int32, (z.tail, z.folded), 0)
    hit = lane == base
    for k in range(1, z.folds):
        hit = hit | (lane == base + k * z.tail)
    spr[...] = one(hit)
    for dst, wide_src, narrow_src in ((rtp, rw_ref, rn_ref), (ltp, lw_ref, ln_ref)):
        dst[0] = jnp.zeros(dst.shape[1:], BF)
        dst[0, : z.cw, : z.wide] = wide_src[...]
        dst[0, : z.cn, z.wide :] = narrow_src[:, : z.beside]
        dst[0, z.cnp : z.cnp + z.cn, z.wide :] = narrow_src[:, z.beside : 2 * z.beside]
        rest = jnp.concatenate(
            [narrow_src[:, 2 * z.beside :].astype(F32), jnp.zeros((z.cnp - z.cn, z.tail), F32)], axis=0
        ).astype(BF)
        kept = jnp.where(in_fold(z.cnp), nn(rest, spr[...]), 0.0).astype(BF)
        to = lax.broadcasted_iota(jnp.int32, (z.cwp, z.cnp), 0)
        frm = lax.broadcasted_iota(jnp.int32, (z.cwp, z.cnp), 1)
        spare_rows = nn(one(to == z.cw + (frm & (z.spare - 1))), kept)
        dst[0, :, : z.folded] = (dst[0, :, : z.folded].astype(F32) + spare_rows).astype(BF)
    spare = jnp.zeros((z.meta - 3 * z.routes, z.tokens), F32)
    meta = jnp.concatenate(
        [gates_ref[...].astype(F32), routes_ref[...].astype(F32), slots_ref[...].astype(F32), spare],
        axis=0,
    ).astype(BF)
    for h in range(2):
        cg[h, 0, 0, 0, : z.meta] = meta
        cg[h, 0, 0, 0, z.meta :] = cot_ref[h * z.part : (h + 1) * z.part]
    wt[...] = jnp.zeros_like(wt)

    pl.semaphore_wait(barrier, 7)

    def gather_copies(kind, direction, step):
        copies = []
        for piece, buf in enumerate(((rtp,), (ltp,))[kind]):
            if direction == 0:
                src, dst = (n - step + 1) % n, n - step
            else:
                src, dst = step - 1, step
            src_ref, dst_ref = buf.at[src], buf.at[dst]
            if step == half:
                middle = buf.shape[1] // 2
                rows = pl.ds(direction * middle, middle)
                src_ref, dst_ref = buf.at[src, rows], buf.at[dst, rows]
            copies.append(pltpu.make_async_remote_copy(
                src_ref=src_ref, dst_ref=dst_ref,
                send_sem=ag_send.at[kind, direction, step - 1, piece],
                recv_sem=ag_recv.at[kind, direction, step - 1, piece],
                device_id=ring_to[direction], device_id_type=MESH,
            ))
        return copies

    def gather_start(kind, step):
        for direction in range(2):
            for copy in gather_copies(kind, direction, step):
                copy.start()

    def gather_step(kind, step):
        for direction in range(2):
            for copy in gather_copies(kind, direction, step):
                copy.wait_recv()
            if step < half:
                for copy in gather_copies(kind, direction, step + 1):
                    copy.start()

    def came_from(direction):
        return side - 1 if direction == 0 else 1

    def share(direction):
        return pl.ds(direction * (z.rows // 2), z.rows // 2)

    def first_copy(h, stage, direction):
        if stage == 0:
            src, dst = cg.at[h, 0, 0, 0], cg.at[h, came_from(direction), 0, 0]
        else:
            src = cg.at[h, came_from(direction), 0, 0, share(direction)]
            dst = cg.at[h, 2, 0, 0, share(direction)]
        return pltpu.make_async_remote_copy(
            src_ref=src, dst_ref=dst,
            send_sem=p_send.at[h, stage, direction], recv_sem=p_recv.at[h, stage, direction],
            device_id=axis_to[h][direction], device_id_type=MESH,
        )

    def second_copy(h, stage, i, direction):
        if stage == 0:
            src, dst = cg.at[h, i, 0, 0], cg.at[h, i, came_from(direction), 0]
        else:
            src = cg.at[h, i, came_from(direction), 0, share(direction)]
            dst = cg.at[h, i, 2, 0, share(direction)]
        return pltpu.make_async_remote_copy(
            src_ref=src, dst_ref=dst,
            send_sem=q_send.at[h, stage, i, direction], recv_sem=q_recv.at[h, stage, i, direction],
            device_id=axis_to[1 - h][direction], device_id_type=MESH,
        )

    def sibling_copy(h, i, j):
        return pltpu.make_async_remote_copy(
            src_ref=cg.at[h, i, j, 0], dst_ref=cg.at[h, i, j, 1],
            send_sem=s_send.at[h, i, j], recv_sem=s_recv.at[h, i, j],
            device_id=sibling, device_id_type=MESH,
        )

    both = tuple((h, d) for d in range(2) for h in range(2))

    def first_arrived():
        for h, d in both:
            first_copy(h, 0, d).wait_recv()
            first_copy(h, 1, d).start()
            i = came_from(d)
            for e in range(2):
                second_copy(h, 0, i, e).start()
            sibling_copy(h, i, 0).start()

    def first_far_arrived():
        for h in range(2):
            for d in range(2):
                first_copy(h, 1, d).wait_recv()
            for e in range(2):
                second_copy(h, 0, 2, e).start()
            sibling_copy(h, 2, 0).start()

    def second_arrived(i):
        for h, d in both:
            second_copy(h, 0, i, d).wait_recv()
            second_copy(h, 1, i, d).start()
            sibling_copy(h, i, came_from(d)).start()

    def second_far_arrived(i):
        for h in range(2):
            for d in range(2):
                second_copy(h, 1, i, d).wait_recv()
            sibling_copy(h, i, 2).start()

    gather_start(0, 1)
    for h, d in both:
        first_copy(h, 0, d).start()
    for h, d in both:
        second_copy(h, 0, 0, d).start()
    gather_start(1, 1)
    for h in range(2):
        sibling_copy(h, 0, 0).start()

    def hidden_wait(k, carry):
        hidden_copy(k).wait()
        return carry

    lax.fori_loop(0, z.experts, hidden_wait, 0)

    def prepare(h, j, place):
        for i in range(side):
            sibling_copy(h, i, j).wait_recv()
        slot_row = lax.broadcasted_iota(jnp.int32, (z.capacity, z.tokens), 0).astype(F32)
        mine = ei.astype(F32)
        for s in range(z.sources):
            info = cg[h, s // 2, j, s % 2, : z.meta].astype(F32)
            weight = jnp.zeros((z.capacity, z.tokens), F32)
            for k in range(z.routes):
                gate = info[k : k + 1]
                route = info[z.routes + k : z.routes + k + 1]
                slot = info[2 * z.routes + k : 2 * z.routes + k + 1]
                weight = weight + jnp.where((route == mine) & (slot == slot_row), gate, 0.0)
            wt[
                s * z.capacity : (s + 1) * z.capacity, s * z.tokens : (s + 1) * z.tokens
            ] = weight.astype(BF)
        left = jnp.concatenate(
            [cg[h, s // 2, j, s % 2, z.meta :, :] for s in range(z.sources)], axis=1
        )
        bt[:, place * z.depth : (place + 1) * z.depth] = nt(left, wt[...]).astype(BF)

    def add_tile(h, offsets, tile, is_first, is_last):
        cols = slice(*z.tiles[tile])
        rows = slice(h * z.part, (h + 1) * z.part)
        size = cols.stop - cols.start
        hidden = jnp.concatenate(
            [(hid_v[:, j, :, :, cols] if h == 0 else hid_v[j, :, :, :, cols]).reshape(z.depth, size)
             for j in offsets], axis=0,
        )
        value = nn(bt[:, : len(offsets) * z.depth], hidden)
        if not is_first:
            value = value + acc[rows, cols]
        if is_last:
            part[rows, cols] = value.astype(BF)
        else:
            acc[rows, cols] = value

    def unpack(kind, first, count):
        src, dst = ((rtp, rtn), (ltp, ltn))[kind]
        some = slice(first, first + count)
        dst[some, :, : z.beside] = src[some, : z.cnp, z.wide :]
        dst[some, :, z.beside : 2 * z.beside] = src[some, z.cnp :, z.wide :]
        to = lax.broadcasted_iota(jnp.int32, (count * z.cnp, count * z.cwp), 0)
        frm = lax.broadcasted_iota(jnp.int32, (count * z.cnp, count * z.cwp), 1)
        same = lax.shift_right_logical(to, z.cnp.bit_length() - 1) == lax.shift_right_logical(
            frm, z.cwp.bit_length() - 1
        )
        pick = same & ((frm & (z.cwp - 1)) == z.cw + (to & (z.spare - 1)))
        rows = nn(one(pick), src[some, :, : z.folded].reshape(count * z.cwp, z.folded))
        rows = jnp.where(in_fold(count * z.cnp), rows, 0.0).astype(BF)
        dst[some, :, 2 * z.beside :] = nt(rows, spr[...]).astype(BF).reshape(count, z.cnp, z.tail)

    def right(first, count):
        for buf, unit, valid, lower, rows in (
            (rtp, z.cwp, z.cw, slice(0, z.wide), slice(0, z.cwp)),
            (rtn, z.cnp, z.cn, slice(z.wide, z.width), slice(z.cwp, z.seg)),
        ):
            depth = lower.stop - lower.start
            left = buf[first : first + count, :, :depth].reshape(count * unit, depth)
            if buf is rtp:
                row = lax.broadcasted_iota(jnp.int32, (count * unit, depth), 0) & (unit - 1)
                left = jnp.where(row < valid, left.astype(F32), 0.0).astype(BF)
            tail = nn(left, part[lower, slice(*z.tiles[2])]).astype(BF)
            keep = z.kept - z.tiles[2][0]
            ht[first : first + count, rows, z.tiles[2][0] : z.kept] = tail[:, :keep].reshape(
                count, unit, keep
            )
            folded = fold(tail[:, keep:], count * unit, unit, valid)
            for tile in range(2):
                cols = slice(*z.tiles[tile])
                value = nn(left, part[lower, cols])
                if tile == 0:
                    value = value + folded
                ht[first : first + count, rows, cols] = value.astype(BF).reshape(
                    count, unit, cols.stop - cols.start
                )

    def spread(size):
        lane = lax.broadcasted_iota(jnp.int32, (z.rest, size), 1)
        return (lane & (z.rest - 1)) == lax.broadcasted_iota(jnp.int32, (z.rest, size), 0)

    def fold(rest, count, unit, valid):
        size = z.tiles[0][1]
        spare = unit - valid
        low = spare.bit_length() - 1
        shift = z.rest.bit_length() - 1
        wide = nn(rest, one(spread(size)))
        row = lax.broadcasted_iota(jnp.int32, (count, size), 0)
        lane = lax.broadcasted_iota(jnp.int32, (count, size), 1)
        own = lax.shift_right_logical(row & (unit - 1), low) == lax.shift_right_logical(lane, shift)
        wide = jnp.where(own, wide, 0.0).astype(BF)
        to = lax.broadcasted_iota(jnp.int32, (count, count), 0)
        frm = lax.broadcasted_iota(jnp.int32, (count, count), 1)
        same = (to & -unit) == (frm & -unit)
        pick = same & ((to & (unit - 1)) - valid == (frm & (spare - 1)))
        return nn(one(pick), wide)

    def unfold(final):
        size = z.tiles[0][1]
        shift = z.rest.bit_length() - 1
        spare_w, spare_n = z.cwp - z.cw, z.cnp - z.cn
        low_w, low_n = spare_w.bit_length() - 1, spare_n.bit_length() - 1
        to = lax.broadcasted_iota(jnp.int32, (z.seg, z.seg), 0)
        frm = lax.broadcasted_iota(jnp.int32, (z.seg, z.seg), 1)
        source = jnp.where(
            to < z.cwp, z.cw + (to & (spare_w - 1)), z.cwp + z.cn + (to & (spare_n - 1))
        )
        rows = nn(one(frm == source), final[:, :size])
        row = lax.broadcasted_iota(jnp.int32, (z.seg, size), 0)
        lane = lax.broadcasted_iota(jnp.int32, (z.seg, size), 1)
        place = jnp.where(
            row < z.cwp,
            lax.shift_right_logical(row, low_w),
            lax.shift_right_logical(row - z.cwp, low_n),
        )
        rows = jnp.where(place == lax.shift_right_logical(lane, shift), rows, 0.0).astype(BF)
        return nt(rows, one(spread(size))).astype(BF)

    middle = z.seg // 2

    def hops(direction, piece):
        return half if direction == piece else half - 1

    def own_slot(direction, distance):
        return distance if direction == 0 else (n - distance) % n

    def reduce_copy(direction, piece, hop):
        rows = pl.ds(piece * middle, middle)
        if hop == 1:
            src = ht.at[own_slot(direction, hops(direction, piece)), rows]
        else:
            src = land.at[direction, hop - 2, rows]
        return pltpu.make_async_remote_copy(
            src_ref=src, dst_ref=land.at[direction, hop - 1, rows],
            send_sem=rs_send.at[direction, piece, hop - 1],
            recv_sem=rs_recv.at[direction, piece, hop - 1],
            device_id=ring_to[direction], device_id_type=MESH,
        )

    lanes = ((0, 1), (1, 0), (0, 0), (1, 1))

    def reduce_step(hop):
        for direction, piece in lanes:
            if hop >= hops(direction, piece):
                continue
            reduce_copy(direction, piece, hop).wait_recv()
            rows = slice(piece * middle, (piece + 1) * middle)
            slot = own_slot(direction, hops(direction, piece) - hop)
            total = land[direction, hop - 1, rows].astype(F32) + ht[slot, rows].astype(F32)
            land[direction, hop - 1, rows] = total.astype(BF)
            reduce_copy(direction, piece, hop + 1).start()

    def compact(dst, src, unit, valid, m):
        shift = unit.bit_length() - 1
        depth = n * unit
        rows = slice(m * z.pick, (m + 1) * z.pick)
        feature = lax.broadcasted_iota(jnp.int32, (z.pick, depth), 0) + m * z.pick
        place = lax.broadcasted_iota(jnp.int32, (z.pick, depth), 1)
        owner = (zi + lax.shift_right_logical(place, shift)) & (n - 1)
        inner = place & (unit - 1)
        pick = one((feature == owner * valid + inner) & (inner < valid))
        width = dst.shape[1]
        dst[rows, :] = nn(pick, src[:, :, :width].reshape(depth, width)).astype(BF)

    def work(h, offsets, is_first=False, is_last=False):
        for place, j in enumerate(offsets):
            prepare(h, j, place)
            yield
        for tile in range(3):
            add_tile(h, offsets, tile, is_first, is_last)
            yield

    def run(*steps):
        for entry in steps:
            if isinstance(entry, int):
                for _ in range(entry):
                    next(jobs, None)
            else:
                entry[0](*entry[1:])

    def all_work():
        for h in range(2):
            yield from work(h, (0,), is_first=True)
        for h in range(2):
            yield from work(h, (1, side - 1))
        for h in range(2):
            yield from work(h, (2,), is_last=True)

    jobs = all_work()
    far = side - 1
    ring = gather_step
    run(
        (ring, 0, 1), (first_arrived,), (ring, 1, 1), (second_arrived, 0), (ring, 0, 2),
        (first_far_arrived,), 1, (ring, 1, 2), 3, (second_arrived, far), (ring, 0, 3), 3,
        (ring, 1, 3), 1, (second_arrived, 1), (ring, 0, 4), (unpack, 0, 0, 4), (second_arrived, 2),
        (ring, 1, 4), (unpack, 0, 12, 4),
        (second_far_arrived, 0), 2, (ring, 0, 5), (second_far_arrived, far), 3, (ring, 1, 5),
        (second_far_arrived, 1), 2, (ring, 0, 6), (second_far_arrived, 2), 3, (ring, 1, 6), 4,
        (ring, 0, 7), (unpack, 0, 4, 4), 4,
    )
    right(0, half)
    reduce_copy(0, 1, 1).start()
    gather_step(1, half - 1)
    unpack(0, half + 1, 3)
    right(half + 1, n - half - 1)
    reduce_copy(1, 0, 1).start()
    gather_step(0, half)
    unpack(0, half, 1)
    right(half, 1)
    reduce_copy(0, 0, 1).start()
    reduce_copy(1, 1, 1).start()
    gather_step(1, half)

    later = [(lwc, ltp, z.cwp, z.cw, m) for m in range(z.wide // z.pick)]
    later += [(lnc, ltn, z.cnp, z.cn, m) for m in range(z.narrow // z.pick)]
    for hop in range(1, half):
        reduce_step(hop)
        if hop < 3:
            unpack(1, (hop - 1) * half, half)
        if hop >= 2 and later:
            compact(*later.pop(0))
    for entry in later:
        compact(*entry)

    sums = []
    for piece in range(2):
        rows = slice(piece * middle, (piece + 1) * middle)
        total = ht[0, rows].astype(F32)
        for direction in range(2):
            hop = hops(direction, piece)
            if hop > 0:
                reduce_copy(direction, piece, hop).wait_recv()
                total = total + land[direction, hop - 1, rows].astype(F32)
        sums.append(total.astype(BF))
    final = jnp.concatenate(sums, axis=0)
    upper = nn(final[:, : z.wide], lwc[...])
    lower = nn(final[:, z.wide :], lnc[: z.kept - z.wide]) + nn(unfold(final), lnc[z.kept - z.wide :])
    result = jnp.concatenate([upper, lower], axis=1)
    ow_ref[:, 0, :] = result[: z.cw]
    on_ref[:, 0, :] = result[z.cwp : z.cwp + z.cn]

    for h in range(2):
        for d in range(2):
            for stage in range(2):
                first_copy(h, stage, d).wait_send()
                for i in range(side):
                    second_copy(h, stage, i, d).wait_send()
        for i in range(side):
            for j in range(side):
                sibling_copy(h, i, j).wait_send()
    for kind in range(2):
        for step in range(1, half + 1):
            for direction in range(2):
                for copy in gather_copies(kind, direction, step):
                    copy.wait_send()
    for direction, piece in lanes:
        for hop in range(1, hops(direction, piece) + 1):
            reduce_copy(direction, piece, hop).wait_send()


def body(
    cotangent, gates, routes, slots, saved_hidden, left_wide, left_narrow, right_wide, right_narrow
):
    ring, experts = lax.axis_size("dp"), lax.axis_size("expert")
    capacity, width = saved_hidden.shape[3:]
    z = Sizes(
        ring, experts, capacity, width, left_wide.shape[1], left_narrow.shape[1],
        cotangent.shape[0], gates.shape[1],
    )
    vmem = pl.BlockSpec(memory_space=pltpu.VMEM)
    ow, on = pl.pallas_call(
        functools.partial(kernel, z),
        out_shape=(
            jax.ShapeDtypeStruct((z.cw, 1, z.width), F32),
            jax.ShapeDtypeStruct((z.cn, 1, z.width), F32),
        ),
        in_specs=[vmem] * 4 + [pl.BlockSpec(memory_space=pl.ANY)] + [vmem] * 4,
        out_specs=(vmem, vmem),
        scratch_shapes=[
            pltpu.VMEM((z.side, z.side, 2, capacity, width), BF),
            pltpu.VMEM((2, z.side, z.side, 2, z.rows, z.tokens), BF),
            pltpu.VMEM((z.depth, z.sources * z.tokens), BF),
            pltpu.VMEM((z.part, 2 * z.depth), BF),
            pltpu.VMEM((width, width), F32),
            pltpu.VMEM((width, width), BF),
            pltpu.VMEM((ring, z.cwp, z.packed), BF),
            pltpu.VMEM((ring, z.cnp, z.narrow), BF),
            pltpu.VMEM((ring, z.cwp, z.packed), BF),
            pltpu.VMEM((ring, z.cnp, z.narrow), BF),
            pltpu.VMEM((z.tail, z.folded), BF),
            pltpu.VMEM((ring, z.seg, z.kept), BF),
            pltpu.VMEM((2, z.half, z.seg, z.kept), BF),
            pltpu.VMEM((z.wide, z.wide), BF),
            pltpu.VMEM((z.narrow, z.narrow), BF),
            pltpu.SemaphoreType.DMA((experts,)),
            pltpu.SemaphoreType.DMA((2, 2, 2)),
            pltpu.SemaphoreType.DMA((2, 2, 2)),
            pltpu.SemaphoreType.DMA((2, 2, z.side, 2)),
            pltpu.SemaphoreType.DMA((2, 2, z.side, 2)),
            pltpu.SemaphoreType.DMA((2, z.side, z.side)),
            pltpu.SemaphoreType.DMA((2, z.side, z.side)),
            pltpu.SemaphoreType.DMA((2, 2, z.half, 1)),
            pltpu.SemaphoreType.DMA((2, 2, z.half, 1)),
            pltpu.SemaphoreType.DMA((2, 2, z.half)),
            pltpu.SemaphoreType.DMA((2, 2, z.half)),
        ],
        compiler_params=pltpu.CompilerParams(
            collective_id=0, has_side_effects=True, vmem_limit_bytes=60 * 1024 * 1024
        ),
        cost_estimate=pl.CostEstimate(flops=10_000_000_000, bytes_accessed=8_000_000, transcendentals=0),
    )(
        cotangent.T, gates.T, routes.T, slots.T,
        saved_hidden.reshape(experts, capacity, width),
        left_wide[0].T, left_narrow[0].T, right_wide[0].T, right_narrow[0].T,
    )
    return jnp.transpose(ow, (1, 2, 0)), jnp.transpose(on, (1, 2, 0))


def solution(mesh):
    return jax.shard_map(
        body,
        mesh=mesh,
        in_specs=(
            P(("dp", "expert"), None),
            P(("dp", "expert"), None),
            P(("dp", "expert"), None),
            P(("dp", "expert"), None),
            P("dp", "expert", None, None, None),
            P("expert", None, "dp"),
            P("expert", None, "dp"),
            P("expert", None, "dp"),
            P("expert", None, "dp"),
        ),
        out_specs=(P("expert", None, "dp"), P("expert", None, "dp")),
        check_vma=False,
    )
```

```python
import functools
import math

import jax
import jax.numpy as jnp
from jax import lax
from jax.experimental import pallas as pl
from jax.experimental.pallas import tpu as pltpu
from jax.sharding import PartitionSpec as P

MESH = pl.DeviceIdType.MESH
BF = jnp.bfloat16
F32 = jnp.float32
LANE = 128


def up(value, unit):
    return -(-value // unit) * unit


def nn(left, right):
    return lax.dot_general(left, right, (((1,), (0,)), ((), ())), preferred_element_type=F32)


def nt(left, right):
    return lax.dot_general(left, right, (((1,), (1,)), ((), ())), preferred_element_type=F32)


class Sizes:
    def __init__(self, ring, experts, capacity, width, wide, narrow, tokens, routes):
        self.ring, self.experts, self.capacity = ring, experts, capacity
        self.width, self.wide, self.narrow = width, wide, narrow
        self.tokens, self.routes = tokens, routes
        self.cw, self.cn = wide // ring, narrow // ring
        self.cwp, self.cnp = up(self.cw, 32), up(self.cn, 32)
        self.seg = self.cwp + self.cnp
        self.half = ring // 2
        self.side = math.isqrt(experts // 2)
        self.part = width // 2
        self.meta = up(3 * routes, 16)
        self.rows = self.meta + self.part
        self.sources = 2 * self.side
        self.depth = self.sources * capacity
        self.rest = width % LANE
        self.kept = width - self.rest
        self.tiles = ((0, 512), (512, 1024), (1024, width))
        self.pick = narrow // 2
        self.beside = 2 * narrow // 5
        self.tail = narrow - 2 * self.beside
        self.packed = wide + self.beside
        self.spare = self.cwp - self.cw
        self.folds = self.cnp // self.spare
        self.folded = self.folds * self.tail


def kernel(
    z, cot_ref, gates_ref, routes_ref, slots_ref, hid_hbm, lw_ref, ln_ref, rw_ref, rn_ref,
    ow_ref, on_ref,
    hid_v, cg, wt, bt, acc, part, rtp, rtn, ltp, ltn, spr, ht, land, lwc, lnc,
    hid_sem, p_send, p_recv, q_send, q_recv, s_send, s_recv, ag_send, ag_recv, rs_send, rs_recv,
):
    n, half, side = z.ring, z.half, z.side
    zi = lax.axis_index("dp")
    ei = lax.axis_index("expert")
    core = lax.rem(ei, 2)
    yi = lax.rem(ei // 2, side)
    xi = ei // (2 * side)

    def expert_at(x, y, c):
        return (x * side + y) * 2 + c

    def step_to(index, direction):
        return lax.rem(index + (1 if direction == 0 else side - 1), side)

    ring_to = ((lax.rem(zi + 1, n), ei), (lax.rem(zi + n - 1, n), ei))
    x_to = tuple((zi, expert_at(step_to(xi, d), yi, core)) for d in range(2))
    y_to = tuple((zi, expert_at(xi, step_to(yi, d), core)) for d in range(2))
    sibling = (zi, expert_at(xi, yi, 1 - core))
    axis_to = (x_to, y_to)

    barrier = pltpu.get_barrier_semaphore()
    for target in (*ring_to, *x_to, *y_to, sibling):
        pl.semaphore_signal(barrier, inc=1, device_id=target, device_id_type=MESH)

    def one(mask):
        return jnp.where(mask, 1.0, 0.0).astype(BF)

    def in_fold(count):
        row = lax.broadcasted_iota(jnp.int32, (count, z.folded), 0) & (z.cnp - 1)
        lane = lax.broadcasted_iota(jnp.int32, (count, z.folded), 1)
        low = lax.shift_right_logical(row, z.spare.bit_length() - 1) * z.tail
        return (lane >= low) & (lane < low + z.tail)

    def hidden_copy(k):
        dx, dy, dc = k // (2 * side), lax.rem(k // 2, side), lax.rem(k, 2)
        source = expert_at(
            lax.rem(xi + dx, side), lax.rem(yi + dy, side), lax.rem(core + dc, 2)
        )
        return pltpu.make_async_copy(hid_hbm.at[source], hid_v.at[dx, dy, dc], hid_sem.at[k])

    def hidden_start(k, carry):
        hidden_copy(k).start()
        return carry

    lax.fori_loop(0, z.experts, hidden_start, 0)

    lane = lax.broadcasted_iota(jnp.int32, (z.tail, z.folded), 1)
    base = lax.broadcasted_iota(jnp.int32, (z.tail, z.folded), 0)
    hit = lane == base
    for k in range(1, z.folds):
        hit = hit | (lane == base + k * z.tail)
    spr[...] = one(hit)
    for dst, wide_src, narrow_src in ((rtp, rw_ref, rn_ref), (ltp, lw_ref, ln_ref)):
        dst[0] = jnp.zeros(dst.shape[1:], BF)
        dst[0, : z.cw, : z.wide] = wide_src[...]
        dst[0, : z.cn, z.wide :] = narrow_src[:, : z.beside]
        dst[0, z.cnp : z.cnp + z.cn, z.wide :] = narrow_src[:, z.beside : 2 * z.beside]
        rest = jnp.concatenate(
            [narrow_src[:, 2 * z.beside :].astype(F32), jnp.zeros((z.cnp - z.cn, z.tail), F32)], axis=0
        ).astype(BF)
        kept = jnp.where(in_fold(z.cnp), nn(rest, spr[...]), 0.0).astype(BF)
        to = lax.broadcasted_iota(jnp.int32, (z.cwp, z.cnp), 0)
        frm = lax.broadcasted_iota(jnp.int32, (z.cwp, z.cnp), 1)
        spare_rows = nn(one(to == z.cw + (frm & (z.spare - 1))), kept)
        dst[0, :, : z.folded] = (dst[0, :, : z.folded].astype(F32) + spare_rows).astype(BF)
    spare = jnp.zeros((z.meta - 3 * z.routes, z.tokens), F32)
    meta = jnp.concatenate(
        [gates_ref[...].astype(F32), routes_ref[...].astype(F32), slots_ref[...].astype(F32), spare],
        axis=0,
    ).astype(BF)
    for h in range(2):
        cg[h, 0, 0, 0, : z.meta] = meta
        cg[h, 0, 0, 0, z.meta :] = cot_ref[h * z.part : (h + 1) * z.part]
    wt[...] = jnp.zeros_like(wt)

    pl.semaphore_wait(barrier, 7)

    def gather_copies(kind, direction, step):
        copies = []
        for piece, buf in enumerate(((rtp,), (ltp,))[kind]):
            if direction == 0:
                src, dst = (n - step + 1) % n, n - step
            else:
                src, dst = step - 1, step
            src_ref, dst_ref = buf.at[src], buf.at[dst]
            if step == half:
                middle = buf.shape[1] // 2
                rows = pl.ds(direction * middle, middle)
                src_ref, dst_ref = buf.at[src, rows], buf.at[dst, rows]
            copies.append(pltpu.make_async_remote_copy(
                src_ref=src_ref, dst_ref=dst_ref,
                send_sem=ag_send.at[kind, direction, step - 1, piece],
                recv_sem=ag_recv.at[kind, direction, step - 1, piece],
                device_id=ring_to[direction], device_id_type=MESH,
            ))
        return copies

    def gather_start(kind, step):
        for direction in range(2):
            for copy in gather_copies(kind, direction, step):
                copy.start()

    def gather_step(kind, step):
        for direction in range(2):
            for copy in gather_copies(kind, direction, step):
                copy.wait_recv()
            if step < half:
                for copy in gather_copies(kind, direction, step + 1):
                    copy.start()

    def came_from(direction):
        return side - 1 if direction == 0 else 1

    def share(direction):
        return pl.ds(direction * (z.rows // 2), z.rows // 2)

    def first_copy(h, stage, direction):
        if stage == 0:
            src, dst = cg.at[h, 0, 0, 0], cg.at[h, came_from(direction), 0, 0]
        else:
            src = cg.at[h, came_from(direction), 0, 0, share(direction)]
            dst = cg.at[h, 2, 0, 0, share(direction)]
        return pltpu.make_async_remote_copy(
            src_ref=src, dst_ref=dst,
            send_sem=p_send.at[h, stage, direction], recv_sem=p_recv.at[h, stage, direction],
            device_id=axis_to[h][direction], device_id_type=MESH,
        )

    def second_copy(h, stage, i, direction):
        if stage == 0:
            src, dst = cg.at[h, i, 0, 0], cg.at[h, i, came_from(direction), 0]
        else:
            src = cg.at[h, i, came_from(direction), 0, share(direction)]
            dst = cg.at[h, i, 2, 0, share(direction)]
        return pltpu.make_async_remote_copy(
            src_ref=src, dst_ref=dst,
            send_sem=q_send.at[h, stage, i, direction], recv_sem=q_recv.at[h, stage, i, direction],
            device_id=axis_to[1 - h][direction], device_id_type=MESH,
        )

    def sibling_copy(h, i, j):
        return pltpu.make_async_remote_copy(
            src_ref=cg.at[h, i, j, 0], dst_ref=cg.at[h, i, j, 1],
            send_sem=s_send.at[h, i, j], recv_sem=s_recv.at[h, i, j],
            device_id=sibling, device_id_type=MESH,
        )

    both = tuple((h, d) for d in range(2) for h in range(2))

    def first_arrived():
        for h, d in both:
            first_copy(h, 0, d).wait_recv()
            first_copy(h, 1, d).start()
            i = came_from(d)
            for e in range(2):
                second_copy(h, 0, i, e).start()
            sibling_copy(h, i, 0).start()

    def first_far_arrived():
        for h in range(2):
            for d in range(2):
                first_copy(h, 1, d).wait_recv()
            for e in range(2):
                second_copy(h, 0, 2, e).start()
            sibling_copy(h, 2, 0).start()

    def second_arrived(i):
        for h, d in both:
            second_copy(h, 0, i, d).wait_recv()
            second_copy(h, 1, i, d).start()
            sibling_copy(h, i, came_from(d)).start()

    def second_far_arrived(i):
        for h in range(2):
            for d in range(2):
                second_copy(h, 1, i, d).wait_recv()
            sibling_copy(h, i, 2).start()

    gather_start(0, 1)
    for h, d in both:
        first_copy(h, 0, d).start()
    for h, d in both:
        second_copy(h, 0, 0, d).start()
    gather_start(1, 1)
    for h in range(2):
        sibling_copy(h, 0, 0).start()

    def hidden_wait(k, carry):
        hidden_copy(k).wait()
        return carry

    lax.fori_loop(0, z.experts, hidden_wait, 0)

    def prepare(h, j, place):
        for i in range(side):
            sibling_copy(h, i, j).wait_recv()
        slot_row = lax.broadcasted_iota(jnp.int32, (z.capacity, z.tokens), 0).astype(F32)
        mine = ei.astype(F32)
        for s in range(z.sources):
            info = cg[h, s // 2, j, s % 2, : z.meta].astype(F32)
            weight = jnp.zeros((z.capacity, z.tokens), F32)
            for k in range(z.routes):
                gate = info[k : k + 1]
                route = info[z.routes + k : z.routes + k + 1]
                slot = info[2 * z.routes + k : 2 * z.routes + k + 1]
                weight = weight + jnp.where((route == mine) & (slot == slot_row), gate, 0.0)
            wt[
                s * z.capacity : (s + 1) * z.capacity, s * z.tokens : (s + 1) * z.tokens
            ] = weight.astype(BF)
        left = jnp.concatenate(
            [cg[h, s // 2, j, s % 2, z.meta :, :] for s in range(z.sources)], axis=1
        )
        bt[:, place * z.depth : (place + 1) * z.depth] = nt(left, wt[...]).astype(BF)

    def add_tile(h, offsets, tile, is_first, is_last):
        cols = slice(*z.tiles[tile])
        rows = slice(h * z.part, (h + 1) * z.part)
        size = cols.stop - cols.start
        hidden = jnp.concatenate(
            [(hid_v[:, j, :, :, cols] if h == 0 else hid_v[j, :, :, :, cols]).reshape(z.depth, size)
             for j in offsets], axis=0,
        )
        value = nn(bt[:, : len(offsets) * z.depth], hidden)
        if not is_first:
            value = value + acc[rows, cols]
        if is_last:
            part[rows, cols] = value.astype(BF)
        else:
            acc[rows, cols] = value

    def unpack(kind, first, count):
        src, dst = ((rtp, rtn), (ltp, ltn))[kind]
        some = slice(first, first + count)
        dst[some, :, : z.beside] = src[some, : z.cnp, z.wide :]
        dst[some, :, z.beside : 2 * z.beside] = src[some, z.cnp :, z.wide :]
        to = lax.broadcasted_iota(jnp.int32, (count * z.cnp, count * z.cwp), 0)
        frm = lax.broadcasted_iota(jnp.int32, (count * z.cnp, count * z.cwp), 1)
        same = lax.shift_right_logical(to, z.cnp.bit_length() - 1) == lax.shift_right_logical(
            frm, z.cwp.bit_length() - 1
        )
        pick = same & ((frm & (z.cwp - 1)) == z.cw + (to & (z.spare - 1)))
        rows = nn(one(pick), src[some, :, : z.folded].reshape(count * z.cwp, z.folded))
        rows = jnp.where(in_fold(count * z.cnp), rows, 0.0).astype(BF)
        dst[some, :, 2 * z.beside :] = nt(rows, spr[...]).astype(BF).reshape(count, z.cnp, z.tail)

    def right(first, count):
        for buf, unit, valid, lower, rows in (
            (rtp, z.cwp, z.cw, slice(0, z.wide), slice(0, z.cwp)),
            (rtn, z.cnp, z.cn, slice(z.wide, z.width), slice(z.cwp, z.seg)),
        ):
            depth = lower.stop - lower.start
            left = buf[first : first + count, :, :depth].reshape(count * unit, depth)
            if buf is rtp:
                row = lax.broadcasted_iota(jnp.int32, (count * unit, depth), 0) & (unit - 1)
                left = jnp.where(row < valid, left.astype(F32), 0.0).astype(BF)
            tail = nn(left, part[lower, slice(*z.tiles[2])]).astype(BF)
            keep = z.kept - z.tiles[2][0]
            ht[first : first + count, rows, z.tiles[2][0] : z.kept] = tail[:, :keep].reshape(
                count, unit, keep
            )
            folded = fold(tail[:, keep:], count * unit, unit, valid)
            for tile in range(2):
                cols = slice(*z.tiles[tile])
                value = nn(left, part[lower, cols])
                if tile == 0:
                    value = value + folded
                ht[first : first + count, rows, cols] = value.astype(BF).reshape(
                    count, unit, cols.stop - cols.start
                )

    def spread(size):
        lane = lax.broadcasted_iota(jnp.int32, (z.rest, size), 1)
        return (lane & (z.rest - 1)) == lax.broadcasted_iota(jnp.int32, (z.rest, size), 0)

    def fold(rest, count, unit, valid):
        size = z.tiles[0][1]
        spare = unit - valid
        low = spare.bit_length() - 1
        shift = z.rest.bit_length() - 1
        wide = nn(rest, one(spread(size)))
        row = lax.broadcasted_iota(jnp.int32, (count, size), 0)
        lane = lax.broadcasted_iota(jnp.int32, (count, size), 1)
        own = lax.shift_right_logical(row & (unit - 1), low) == lax.shift_right_logical(lane, shift)
        wide = jnp.where(own, wide, 0.0).astype(BF)
        to = lax.broadcasted_iota(jnp.int32, (count, count), 0)
        frm = lax.broadcasted_iota(jnp.int32, (count, count), 1)
        same = (to & -unit) == (frm & -unit)
        pick = same & ((to & (unit - 1)) - valid == (frm & (spare - 1)))
        return nn(one(pick), wide)

    def unfold(final):
        size = z.tiles[0][1]
        shift = z.rest.bit_length() - 1
        spare_w, spare_n = z.cwp - z.cw, z.cnp - z.cn
        low_w, low_n = spare_w.bit_length() - 1, spare_n.bit_length() - 1
        to = lax.broadcasted_iota(jnp.int32, (z.seg, z.seg), 0)
        frm = lax.broadcasted_iota(jnp.int32, (z.seg, z.seg), 1)
        source = jnp.where(
            to < z.cwp, z.cw + (to & (spare_w - 1)), z.cwp + z.cn + (to & (spare_n - 1))
        )
        rows = nn(one(frm == source), final[:, :size])
        row = lax.broadcasted_iota(jnp.int32, (z.seg, size), 0)
        lane = lax.broadcasted_iota(jnp.int32, (z.seg, size), 1)
        place = jnp.where(
            row < z.cwp,
            lax.shift_right_logical(row, low_w),
            lax.shift_right_logical(row - z.cwp, low_n),
        )
        rows = jnp.where(place == lax.shift_right_logical(lane, shift), rows, 0.0).astype(BF)
        return nt(rows, one(spread(size))).astype(BF)

    middle = z.seg // 2

    def hops(direction, piece):
        return half if direction == piece else half - 1

    def own_slot(direction, distance):
        return distance if direction == 0 else (n - distance) % n

    def reduce_copy(direction, piece, hop):
        rows = pl.ds(piece * middle, middle)
        if hop == 1:
            src = ht.at[own_slot(direction, hops(direction, piece)), rows]
        else:
            src = land.at[direction, hop - 2, rows]
        return pltpu.make_async_remote_copy(
            src_ref=src, dst_ref=land.at[direction, hop - 1, rows],
            send_sem=rs_send.at[direction, piece, hop - 1],
            recv_sem=rs_recv.at[direction, piece, hop - 1],
            device_id=ring_to[direction], device_id_type=MESH,
        )

    lanes = ((0, 1), (1, 0), (0, 0), (1, 1))

    def reduce_step(hop):
        for direction, piece in lanes:
            if hop >= hops(direction, piece):
                continue
            reduce_copy(direction, piece, hop).wait_recv()
            rows = slice(piece * middle, (piece + 1) * middle)
            slot = own_slot(direction, hops(direction, piece) - hop)
            total = land[direction, hop - 1, rows].astype(F32) + ht[slot, rows].astype(F32)
            land[direction, hop - 1, rows] = total.astype(BF)
            reduce_copy(direction, piece, hop + 1).start()

    def compact(dst, src, unit, valid, m):
        shift = unit.bit_length() - 1
        depth = n * unit
        rows = slice(m * z.pick, (m + 1) * z.pick)
        feature = lax.broadcasted_iota(jnp.int32, (z.pick, depth), 0) + m * z.pick
        place = lax.broadcasted_iota(jnp.int32, (z.pick, depth), 1)
        owner = (zi + lax.shift_right_logical(place, shift)) & (n - 1)
        inner = place & (unit - 1)
        pick = one((feature == owner * valid + inner) & (inner < valid))
        width = dst.shape[1]
        dst[rows, :] = nn(pick, src[:, :, :width].reshape(depth, width)).astype(BF)

    def work(h, offsets, is_first=False, is_last=False):
        for place, j in enumerate(offsets):
            prepare(h, j, place)
            yield
        for tile in range(3):
            add_tile(h, offsets, tile, is_first, is_last)
            yield

    def run(*steps):
        for entry in steps:
            if isinstance(entry, int):
                for _ in range(entry):
                    next(jobs, None)
            else:
                entry[0](*entry[1:])

    def all_work():
        for h in range(2):
            yield from work(h, (0,), is_first=True)
        for h in range(2):
            yield from work(h, (1, side - 1))
        for h in range(2):
            yield from work(h, (2,), is_last=True)

    jobs = all_work()
    far = side - 1
    ring = gather_step
    run(
        (ring, 0, 1),
        (ring, 1, 1), (first_arrived,),
        (ring, 0, 2), (second_arrived, 0),
        (ring, 1, 2), (first_far_arrived,), 3,
        (ring, 0, 3), (second_arrived, far), 3,
        (ring, 1, 3), 2,
        (ring, 0, 4), (unpack, 0, 0, 4), (second_arrived, 1),
        (ring, 1, 4), (unpack, 0, 12, 4), (second_arrived, 2), 3,
        (ring, 0, 5), (second_far_arrived, 0), 3,
        (ring, 1, 5), (second_far_arrived, far), 3,
        (ring, 0, 6), (second_far_arrived, 1), 1,
        (ring, 1, 6), (second_far_arrived, 2), 5,
        (ring, 0, 7), (unpack, 0, 4, 4), 3,
    )
    right(0, half)
    reduce_copy(0, 1, 1).start()
    gather_step(1, half - 1)
    unpack(0, half + 1, 3)
    right(half + 1, n - half - 1)
    reduce_copy(1, 0, 1).start()
    gather_step(0, half)
    unpack(0, half, 1)
    right(half, 1)
    reduce_copy(0, 0, 1).start()
    reduce_copy(1, 1, 1).start()
    gather_step(1, half)

    later = [(lwc, ltp, z.cwp, z.cw, m) for m in range(z.wide // z.pick)]
    later += [(lnc, ltn, z.cnp, z.cn, m) for m in range(z.narrow // z.pick)]
    for hop in range(1, half):
        reduce_step(hop)
        if hop < 3:
            unpack(1, (hop - 1) * half, half)
        if hop >= 2 and later:
            compact(*later.pop(0))
    for entry in later:
        compact(*entry)

    sums = []
    for piece in range(2):
        rows = slice(piece * middle, (piece + 1) * middle)
        total = ht[0, rows].astype(F32)
        for direction in range(2):
            hop = hops(direction, piece)
            if hop > 0:
                reduce_copy(direction, piece, hop).wait_recv()
                total = total + land[direction, hop - 1, rows].astype(F32)
        sums.append(total.astype(BF))
    final = jnp.concatenate(sums, axis=0)
    upper = nn(final[:, : z.wide], lwc[...])
    lower = nn(final[:, z.wide :], lnc[: z.kept - z.wide]) + nn(unfold(final), lnc[z.kept - z.wide :])
    result = jnp.concatenate([upper, lower], axis=1)
    ow_ref[:, 0, :] = result[: z.cw]
    on_ref[:, 0, :] = result[z.cwp : z.cwp + z.cn]

    for h in range(2):
        for d in range(2):
            for stage in range(2):
                first_copy(h, stage, d).wait_send()
                for i in range(side):
                    second_copy(h, stage, i, d).wait_send()
        for i in range(side):
            for j in range(side):
                sibling_copy(h, i, j).wait_send()
    for kind in range(2):
        for step in range(1, half + 1):
            for direction in range(2):
                for copy in gather_copies(kind, direction, step):
                    copy.wait_send()
    for direction, piece in lanes:
        for hop in range(1, hops(direction, piece) + 1):
            reduce_copy(direction, piece, hop).wait_send()


def body(
    cotangent, gates, routes, slots, saved_hidden, left_wide, left_narrow, right_wide, right_narrow
):
    ring, experts = lax.axis_size("dp"), lax.axis_size("expert")
    capacity, width = saved_hidden.shape[3:]
    z = Sizes(
        ring, experts, capacity, width, left_wide.shape[1], left_narrow.shape[1],
        cotangent.shape[0], gates.shape[1],
    )
    vmem = pl.BlockSpec(memory_space=pltpu.VMEM)
    ow, on = pl.pallas_call(
        functools.partial(kernel, z),
        out_shape=(
            jax.ShapeDtypeStruct((z.cw, 1, z.width), F32),
            jax.ShapeDtypeStruct((z.cn, 1, z.width), F32),
        ),
        in_specs=[vmem] * 4 + [pl.BlockSpec(memory_space=pl.ANY)] + [vmem] * 4,
        out_specs=(vmem, vmem),
        scratch_shapes=[
            pltpu.VMEM((z.side, z.side, 2, capacity, width), BF),
            pltpu.VMEM((2, z.side, z.side, 2, z.rows, z.tokens), BF),
            pltpu.VMEM((z.depth, z.sources * z.tokens), BF),
            pltpu.VMEM((z.part, 2 * z.depth), BF),
            pltpu.VMEM((width, width), F32),
            pltpu.VMEM((width, width), BF),
            pltpu.VMEM((ring, z.cwp, z.packed), BF),
            pltpu.VMEM((ring, z.cnp, z.narrow), BF),
            pltpu.VMEM((ring, z.cwp, z.packed), BF),
            pltpu.VMEM((ring, z.cnp, z.narrow), BF),
            pltpu.VMEM((z.tail, z.folded), BF),
            pltpu.VMEM((ring, z.seg, z.kept), BF),
            pltpu.VMEM((2, z.half, z.seg, z.kept), BF),
            pltpu.VMEM((z.wide, z.wide), BF),
            pltpu.VMEM((z.narrow, z.narrow), BF),
            pltpu.SemaphoreType.DMA((experts,)),
            pltpu.SemaphoreType.DMA((2, 2, 2)),
            pltpu.SemaphoreType.DMA((2, 2, 2)),
            pltpu.SemaphoreType.DMA((2, 2, z.side, 2)),
            pltpu.SemaphoreType.DMA((2, 2, z.side, 2)),
            pltpu.SemaphoreType.DMA((2, z.side, z.side)),
            pltpu.SemaphoreType.DMA((2, z.side, z.side)),
            pltpu.SemaphoreType.DMA((2, 2, z.half, 1)),
            pltpu.SemaphoreType.DMA((2, 2, z.half, 1)),
            pltpu.SemaphoreType.DMA((2, 2, z.half)),
            pltpu.SemaphoreType.DMA((2, 2, z.half)),
        ],
        compiler_params=pltpu.CompilerParams(
            collective_id=0, has_side_effects=True, vmem_limit_bytes=60 * 1024 * 1024
        ),
        cost_estimate=pl.CostEstimate(flops=10_000_000_000, bytes_accessed=8_000_000, transcendentals=0),
    )(
        cotangent.T, gates.T, routes.T, slots.T,
        saved_hidden.reshape(experts, capacity, width),
        left_wide[0].T, left_narrow[0].T, right_wide[0].T, right_narrow[0].T,
    )
    return jnp.transpose(ow, (1, 2, 0)), jnp.transpose(on, (1, 2, 0))


def solution(mesh):
    return jax.shard_map(
        body,
        mesh=mesh,
        in_specs=(
            P(("dp", "expert"), None),
            P(("dp", "expert"), None),
            P(("dp", "expert"), None),
            P(("dp", "expert"), None),
            P("dp", "expert", None, None, None),
            P("expert", None, "dp"),
            P("expert", None, "dp"),
            P("expert", None, "dp"),
            P("expert", None, "dp"),
        ),
        out_specs=(P("expert", None, "dp"), P("expert", None, "dp")),
        check_vma=False,
    )
```

```python
import functools
import math

import jax
import jax.numpy as jnp
from jax import lax
from jax.experimental import pallas as pl
from jax.experimental.pallas import tpu as pltpu
from jax.sharding import PartitionSpec as P

MESH = pl.DeviceIdType.MESH
BF = jnp.bfloat16
F32 = jnp.float32
LANE = 128


def up(value, unit):
    return -(-value // unit) * unit


def nn(left, right):
    return lax.dot_general(left, right, (((1,), (0,)), ((), ())), preferred_element_type=F32)


def nt(left, right):
    return lax.dot_general(left, right, (((1,), (1,)), ((), ())), preferred_element_type=F32)


class Sizes:
    def __init__(self, ring, experts, capacity, width, wide, narrow, tokens, routes):
        self.ring, self.experts, self.capacity = ring, experts, capacity
        self.width, self.wide, self.narrow = width, wide, narrow
        self.tokens, self.routes = tokens, routes
        self.cw, self.cn = wide // ring, narrow // ring
        self.cwp, self.cnp = up(self.cw, 32), up(self.cn, 32)
        self.seg = self.cwp + self.cnp
        self.half = ring // 2
        self.side = math.isqrt(experts // 2)
        self.part = width // 2
        self.meta = up(3 * routes, 16)
        self.rows = self.meta + self.part
        self.sources = 2 * self.side
        self.depth = self.sources * capacity
        self.rest = width % LANE
        self.kept = width - self.rest
        self.tiles = ((0, 512), (512, 1024), (1024, width))
        self.pick = narrow // 2
        self.beside = 2 * narrow // 5
        self.tail = narrow - 2 * self.beside
        self.packed = wide + self.beside
        self.spare = self.cwp - self.cw
        self.folds = self.cnp // self.spare
        self.folded = self.folds * self.tail


def kernel(
    z, cot_ref, gates_ref, routes_ref, slots_ref, hid_hbm, lw_ref, ln_ref, rw_ref, rn_ref,
    ow_ref, on_ref,
    hid_v, cg, wt, bt, acc, part, rtp, rtn, ltp, ltn, spr, ht, land, lwc, lnc,
    hid_sem, p_send, p_recv, q_send, q_recv, s_send, s_recv, ag_send, ag_recv, rs_send, rs_recv,
):
    n, half, side = z.ring, z.half, z.side
    zi = lax.axis_index("dp")
    ei = lax.axis_index("expert")
    core = lax.rem(ei, 2)
    yi = lax.rem(ei // 2, side)
    xi = ei // (2 * side)

    def expert_at(x, y, c):
        return (x * side + y) * 2 + c

    def step_to(index, direction):
        return lax.rem(index + (1 if direction == 0 else side - 1), side)

    ring_to = ((lax.rem(zi + 1, n), ei), (lax.rem(zi + n - 1, n), ei))
    x_to = tuple((zi, expert_at(step_to(xi, d), yi, core)) for d in range(2))
    y_to = tuple((zi, expert_at(xi, step_to(yi, d), core)) for d in range(2))
    sibling = (zi, expert_at(xi, yi, 1 - core))
    axis_to = (x_to, y_to)

    barrier = pltpu.get_barrier_semaphore()
    for target in (*ring_to, *x_to, *y_to, sibling):
        pl.semaphore_signal(barrier, inc=1, device_id=target, device_id_type=MESH)

    def one(mask):
        return jnp.where(mask, 1.0, 0.0).astype(BF)

    def in_fold(count):
        row = lax.broadcasted_iota(jnp.int32, (count, z.folded), 0) & (z.cnp - 1)
        lane = lax.broadcasted_iota(jnp.int32, (count, z.folded), 1)
        low = lax.shift_right_logical(row, z.spare.bit_length() - 1) * z.tail
        return (lane >= low) & (lane < low + z.tail)

    def hidden_copy(k):
        dx, dy, dc = k // (2 * side), lax.rem(k // 2, side), lax.rem(k, 2)
        source = expert_at(
            lax.rem(xi + dx, side), lax.rem(yi + dy, side), lax.rem(core + dc, 2)
        )
        return pltpu.make_async_copy(hid_hbm.at[source], hid_v.at[dx, dy, dc], hid_sem.at[k])

    def hidden_start(k, carry):
        hidden_copy(k).start()
        return carry

    lax.fori_loop(0, z.experts, hidden_start, 0)

    lane = lax.broadcasted_iota(jnp.int32, (z.tail, z.folded), 1)
    base = lax.broadcasted_iota(jnp.int32, (z.tail, z.folded), 0)
    hit = lane == base
    for k in range(1, z.folds):
        hit = hit | (lane == base + k * z.tail)
    spr[...] = one(hit)
    for dst, wide_src, narrow_src in ((rtp, rw_ref, rn_ref), (ltp, lw_ref, ln_ref)):
        dst[0] = jnp.zeros(dst.shape[1:], BF)
        dst[0, : z.cw, : z.wide] = wide_src[...]
        dst[0, : z.cn, z.wide :] = narrow_src[:, : z.beside]
        dst[0, z.cnp : z.cnp + z.cn, z.wide :] = narrow_src[:, z.beside : 2 * z.beside]
        rest = jnp.concatenate(
            [narrow_src[:, 2 * z.beside :].astype(F32), jnp.zeros((z.cnp - z.cn, z.tail), F32)], axis=0
        ).astype(BF)
        kept = jnp.where(in_fold(z.cnp), nn(rest, spr[...]), 0.0).astype(BF)
        to = lax.broadcasted_iota(jnp.int32, (z.cwp, z.cnp), 0)
        frm = lax.broadcasted_iota(jnp.int32, (z.cwp, z.cnp), 1)
        spare_rows = nn(one(to == z.cw + (frm & (z.spare - 1))), kept)
        dst[0, :, : z.folded] = (dst[0, :, : z.folded].astype(F32) + spare_rows).astype(BF)
    spare = jnp.zeros((z.meta - 3 * z.routes, z.tokens), F32)
    meta = jnp.concatenate(
        [gates_ref[...].astype(F32), routes_ref[...].astype(F32), slots_ref[...].astype(F32), spare],
        axis=0,
    ).astype(BF)
    for h in range(2):
        cg[h, 0, 0, 0, : z.meta] = meta
        cg[h, 0, 0, 0, z.meta :] = cot_ref[h * z.part : (h + 1) * z.part]
    wt[...] = jnp.zeros_like(wt)

    pl.semaphore_wait(barrier, 7)

    def gather_copies(kind, direction, step):
        copies = []
        for piece, buf in enumerate(((rtp,), (ltp,))[kind]):
            if direction == 0:
                src, dst = (n - step + 1) % n, n - step
            else:
                src, dst = step - 1, step
            src_ref, dst_ref = buf.at[src], buf.at[dst]
            if step == half:
                middle = buf.shape[1] // 2
                rows = pl.ds(direction * middle, middle)
                src_ref, dst_ref = buf.at[src, rows], buf.at[dst, rows]
            copies.append(pltpu.make_async_remote_copy(
                src_ref=src_ref, dst_ref=dst_ref,
                send_sem=ag_send.at[kind, direction, step - 1, piece],
                recv_sem=ag_recv.at[kind, direction, step - 1, piece],
                device_id=ring_to[direction], device_id_type=MESH,
            ))
        return copies

    def gather_start(kind, step):
        for direction in range(2):
            for copy in gather_copies(kind, direction, step):
                copy.start()

    def gather_step(kind, step):
        for direction in range(2):
            for copy in gather_copies(kind, direction, step):
                copy.wait_recv()
            if step < half:
                for copy in gather_copies(kind, direction, step + 1):
                    copy.start()

    def came_from(direction):
        return side - 1 if direction == 0 else 1

    def share(direction):
        return pl.ds(direction * (z.rows // 2), z.rows // 2)

    def first_copy(h, stage, direction):
        if stage == 0:
            src, dst = cg.at[h, 0, 0, 0], cg.at[h, came_from(direction), 0, 0]
        else:
            src = cg.at[h, came_from(direction), 0, 0, share(direction)]
            dst = cg.at[h, 2, 0, 0, share(direction)]
        return pltpu.make_async_remote_copy(
            src_ref=src, dst_ref=dst,
            send_sem=p_send.at[h, stage, direction], recv_sem=p_recv.at[h, stage, direction],
            device_id=axis_to[h][direction], device_id_type=MESH,
        )

    def second_copy(h, stage, i, direction):
        if stage == 0:
            src, dst = cg.at[h, i, 0, 0], cg.at[h, i, came_from(direction), 0]
        else:
            src = cg.at[h, i, came_from(direction), 0, share(direction)]
            dst = cg.at[h, i, 2, 0, share(direction)]
        return pltpu.make_async_remote_copy(
            src_ref=src, dst_ref=dst,
            send_sem=q_send.at[h, stage, i, direction], recv_sem=q_recv.at[h, stage, i, direction],
            device_id=axis_to[1 - h][direction], device_id_type=MESH,
        )

    def sibling_copy(h, i, j):
        return pltpu.make_async_remote_copy(
            src_ref=cg.at[h, i, j, 0], dst_ref=cg.at[h, i, j, 1],
            send_sem=s_send.at[h, i, j], recv_sem=s_recv.at[h, i, j],
            device_id=sibling, device_id_type=MESH,
        )

    both = tuple((h, d) for d in range(2) for h in range(2))

    def first_arrived():
        for h, d in both:
            first_copy(h, 0, d).wait_recv()
            first_copy(h, 1, d).start()
            i = came_from(d)
            for e in range(2):
                second_copy(h, 0, i, e).start()
            sibling_copy(h, i, 0).start()

    def first_far_arrived():
        for h in range(2):
            for d in range(2):
                first_copy(h, 1, d).wait_recv()
            for e in range(2):
                second_copy(h, 0, 2, e).start()
            sibling_copy(h, 2, 0).start()

    def second_arrived(i):
        for h, d in both:
            second_copy(h, 0, i, d).wait_recv()
            second_copy(h, 1, i, d).start()
            sibling_copy(h, i, came_from(d)).start()

    def second_far_arrived(i):
        for h in range(2):
            for d in range(2):
                second_copy(h, 1, i, d).wait_recv()
            sibling_copy(h, i, 2).start()

    gather_start(0, 1)
    for h, d in both:
        first_copy(h, 0, d).start()
    for h, d in both:
        second_copy(h, 0, 0, d).start()
    gather_start(1, 1)
    for h in range(2):
        sibling_copy(h, 0, 0).start()

    def hidden_wait(k, carry):
        hidden_copy(k).wait()
        return carry

    lax.fori_loop(0, z.experts, hidden_wait, 0)

    def prepare(h, j, place):
        for i in range(side):
            sibling_copy(h, i, j).wait_recv()
        slot_row = lax.broadcasted_iota(jnp.int32, (z.capacity, z.tokens), 0).astype(F32)
        mine = ei.astype(F32)
        for s in range(z.sources):
            info = cg[h, s // 2, j, s % 2, : z.meta].astype(F32)
            weight = jnp.zeros((z.capacity, z.tokens), F32)
            for k in range(z.routes):
                gate = info[k : k + 1]
                route = info[z.routes + k : z.routes + k + 1]
                slot = info[2 * z.routes + k : 2 * z.routes + k + 1]
                weight = weight + jnp.where((route == mine) & (slot == slot_row), gate, 0.0)
            wt[
                s * z.capacity : (s + 1) * z.capacity, s * z.tokens : (s + 1) * z.tokens
            ] = weight.astype(BF)
        left = jnp.concatenate(
            [cg[h, s // 2, j, s % 2, z.meta :, :] for s in range(z.sources)], axis=1
        )
        bt[:, place * z.depth : (place + 1) * z.depth] = nt(left, wt[...]).astype(BF)

    def add_tile(h, offsets, tile, is_first, is_last):
        cols = slice(*z.tiles[tile])
        rows = slice(h * z.part, (h + 1) * z.part)
        size = cols.stop - cols.start
        hidden = jnp.concatenate(
            [(hid_v[:, j, :, :, cols] if h == 0 else hid_v[j, :, :, :, cols]).reshape(z.depth, size)
             for j in offsets], axis=0,
        )
        value = nn(bt[:, : len(offsets) * z.depth], hidden)
        if not is_first:
            value = value + acc[rows, cols]
        if is_last:
            part[rows, cols] = value.astype(BF)
        else:
            acc[rows, cols] = value

    def unpack(kind, first, count):
        src, dst = ((rtp, rtn), (ltp, ltn))[kind]
        some = slice(first, first + count)
        dst[some, :, : z.beside] = src[some, : z.cnp, z.wide :]
        dst[some, :, z.beside : 2 * z.beside] = src[some, z.cnp :, z.wide :]
        to = lax.broadcasted_iota(jnp.int32, (count * z.cnp, count * z.cwp), 0)
        frm = lax.broadcasted_iota(jnp.int32, (count * z.cnp, count * z.cwp), 1)
        same = lax.shift_right_logical(to, z.cnp.bit_length() - 1) == lax.shift_right_logical(
            frm, z.cwp.bit_length() - 1
        )
        pick = same & ((frm & (z.cwp - 1)) == z.cw + (to & (z.spare - 1)))
        rows = nn(one(pick), src[some, :, : z.folded].reshape(count * z.cwp, z.folded))
        rows = jnp.where(in_fold(count * z.cnp), rows, 0.0).astype(BF)
        dst[some, :, 2 * z.beside :] = nt(rows, spr[...]).astype(BF).reshape(count, z.cnp, z.tail)

    def right(first, count):
        for buf, unit, valid, lower, rows in (
            (rtp, z.cwp, z.cw, slice(0, z.wide), slice(0, z.cwp)),
            (rtn, z.cnp, z.cn, slice(z.wide, z.width), slice(z.cwp, z.seg)),
        ):
            depth = lower.stop - lower.start
            left = buf[first : first + count, :, :depth].reshape(count * unit, depth)
            if buf is rtp:
                row = lax.broadcasted_iota(jnp.int32, (count * unit, depth), 0) & (unit - 1)
                left = jnp.where(row < valid, left.astype(F32), 0.0).astype(BF)
            tail = nn(left, part[lower, slice(*z.tiles[2])]).astype(BF)
            keep = z.kept - z.tiles[2][0]
            ht[first : first + count, rows, z.tiles[2][0] : z.kept] = tail[:, :keep].reshape(
                count, unit, keep
            )
            folded = fold(tail[:, keep:], count * unit, unit, valid)
            for tile in range(2):
                cols = slice(*z.tiles[tile])
                value = nn(left, part[lower, cols])
                if tile == 0:
                    value = value + folded
                ht[first : first + count, rows, cols] = value.astype(BF).reshape(
                    count, unit, cols.stop - cols.start
                )

    def spread(size):
        lane = lax.broadcasted_iota(jnp.int32, (z.rest, size), 1)
        return (lane & (z.rest - 1)) == lax.broadcasted_iota(jnp.int32, (z.rest, size), 0)

    def fold(rest, count, unit, valid):
        size = z.tiles[0][1]
        spare = unit - valid
        low = spare.bit_length() - 1
        shift = z.rest.bit_length() - 1
        wide = nn(rest, one(spread(size)))
        row = lax.broadcasted_iota(jnp.int32, (count, size), 0)
        lane = lax.broadcasted_iota(jnp.int32, (count, size), 1)
        own = lax.shift_right_logical(row & (unit - 1), low) == lax.shift_right_logical(lane, shift)
        wide = jnp.where(own, wide, 0.0).astype(BF)
        to = lax.broadcasted_iota(jnp.int32, (count, count), 0)
        frm = lax.broadcasted_iota(jnp.int32, (count, count), 1)
        same = (to & -unit) == (frm & -unit)
        pick = same & ((to & (unit - 1)) - valid == (frm & (spare - 1)))
        return nn(one(pick), wide)

    def unfold(final):
        size = z.tiles[0][1]
        shift = z.rest.bit_length() - 1
        spare_w, spare_n = z.cwp - z.cw, z.cnp - z.cn
        low_w, low_n = spare_w.bit_length() - 1, spare_n.bit_length() - 1
        to = lax.broadcasted_iota(jnp.int32, (z.seg, z.seg), 0)
        frm = lax.broadcasted_iota(jnp.int32, (z.seg, z.seg), 1)
        source = jnp.where(
            to < z.cwp, z.cw + (to & (spare_w - 1)), z.cwp + z.cn + (to & (spare_n - 1))
        )
        rows = nn(one(frm == source), final[:, :size])
        row = lax.broadcasted_iota(jnp.int32, (z.seg, size), 0)
        lane = lax.broadcasted_iota(jnp.int32, (z.seg, size), 1)
        place = jnp.where(
            row < z.cwp,
            lax.shift_right_logical(row, low_w),
            lax.shift_right_logical(row - z.cwp, low_n),
        )
        rows = jnp.where(place == lax.shift_right_logical(lane, shift), rows, 0.0).astype(BF)
        return nt(rows, one(spread(size))).astype(BF)

    middle = z.seg // 2

    def hops(direction, piece):
        return half if direction == piece else half - 1

    def own_slot(direction, distance):
        return distance if direction == 0 else (n - distance) % n

    def reduce_copy(direction, piece, hop):
        rows = pl.ds(piece * middle, middle)
        if hop == 1:
            src = ht.at[own_slot(direction, hops(direction, piece)), rows]
        else:
            src = land.at[direction, hop - 2, rows]
        return pltpu.make_async_remote_copy(
            src_ref=src, dst_ref=land.at[direction, hop - 1, rows],
            send_sem=rs_send.at[direction, piece, hop - 1],
            recv_sem=rs_recv.at[direction, piece, hop - 1],
            device_id=ring_to[direction], device_id_type=MESH,
        )

    lanes = ((0, 1), (1, 0), (0, 0), (1, 1))

    def reduce_step(hop):
        for direction, piece in lanes:
            if hop >= hops(direction, piece):
                continue
            reduce_copy(direction, piece, hop).wait_recv()
            rows = slice(piece * middle, (piece + 1) * middle)
            slot = own_slot(direction, hops(direction, piece) - hop)
            total = land[direction, hop - 1, rows].astype(F32) + ht[slot, rows].astype(F32)
            land[direction, hop - 1, rows] = total.astype(BF)
            reduce_copy(direction, piece, hop + 1).start()

    def compact(dst, src, unit, valid, m):
        shift = unit.bit_length() - 1
        depth = n * unit
        rows = slice(m * z.pick, (m + 1) * z.pick)
        feature = lax.broadcasted_iota(jnp.int32, (z.pick, depth), 0) + m * z.pick
        place = lax.broadcasted_iota(jnp.int32, (z.pick, depth), 1)
        owner = (zi + lax.shift_right_logical(place, shift)) & (n - 1)
        inner = place & (unit - 1)
        pick = one((feature == owner * valid + inner) & (inner < valid))
        width = dst.shape[1]
        dst[rows, :] = nn(pick, src[:, :, :width].reshape(depth, width)).astype(BF)

    def work(h, offsets, is_first=False, is_last=False):
        for place, j in enumerate(offsets):
            prepare(h, j, place)
            yield
        for tile in range(3):
            add_tile(h, offsets, tile, is_first, is_last)
            yield

    def run(*steps):
        for entry in steps:
            if isinstance(entry, int):
                for _ in range(entry):
                    next(jobs, None)
            else:
                entry[0](*entry[1:])

    def all_work():
        for h in range(2):
            yield from work(h, (0,), is_first=True)
        for h in range(2):
            yield from work(h, (1, side - 1))
        for h in range(2):
            yield from work(h, (2,), is_last=True)

    jobs = all_work()
    far = side - 1
    ring = gather_step
    run(
        (ring, 0, 1), (first_arrived,), (ring, 1, 1), (second_arrived, 0), (ring, 0, 2),
        (first_far_arrived,), 1, (ring, 1, 2), 3, (second_arrived, far), (ring, 0, 3), 3,
        (ring, 1, 3), 1, (second_arrived, 1), (ring, 0, 4), (unpack, 0, 0, 4), (second_arrived, 2),
        (ring, 1, 4), (unpack, 0, 12, 4),
        (second_far_arrived, 0), 2, (ring, 0, 5), (second_far_arrived, far), 3, (ring, 1, 5),
        (second_far_arrived, 1), 2, (ring, 0, 6), (second_far_arrived, 2), 3, (ring, 1, 6), 4,
        (ring, 0, 7), (unpack, 0, 4, 4), 4,
    )
    gather_step(0, half)
    unpack(0, half, 4)
    gather_step(1, half - 1)
    right(half - 2, 5)
    for direction, piece in lanes:
        reduce_copy(direction, piece, 1).start()
    gather_step(1, half)
    right(half + 3, n - half - 3)

    later = [(lwc, ltp, z.cwp, z.cw, m) for m in range(z.wide // z.pick)]
    later += [(lnc, ltn, z.cnp, z.cn, m) for m in range(z.narrow // z.pick)]
    for hop in range(1, half):
        reduce_step(hop)
        if hop == 1:
            right(0, half - 2)
        if 1 < hop < 4:
            unpack(1, (hop - 2) * half, half)
        if hop >= 2 and later:
            compact(*later.pop(0))
    for entry in later:
        compact(*entry)

    sums = []
    for piece in range(2):
        rows = slice(piece * middle, (piece + 1) * middle)
        total = ht[0, rows].astype(F32)
        for direction in range(2):
            hop = hops(direction, piece)
            if hop > 0:
                reduce_copy(direction, piece, hop).wait_recv()
                total = total + land[direction, hop - 1, rows].astype(F32)
        sums.append(total.astype(BF))
    final = jnp.concatenate(sums, axis=0)
    upper = nn(final[:, : z.wide], lwc[...])
    lower = nn(final[:, z.wide :], lnc[: z.kept - z.wide]) + nn(unfold(final), lnc[z.kept - z.wide :])
    result = jnp.concatenate([upper, lower], axis=1)
    ow_ref[:, 0, :] = result[: z.cw]
    on_ref[:, 0, :] = result[z.cwp : z.cwp + z.cn]

    for h in range(2):
        for d in range(2):
            for stage in range(2):
                first_copy(h, stage, d).wait_send()
                for i in range(side):
                    second_copy(h, stage, i, d).wait_send()
        for i in range(side):
            for j in range(side):
                sibling_copy(h, i, j).wait_send()
    for kind in range(2):
        for step in range(1, half + 1):
            for direction in range(2):
                for copy in gather_copies(kind, direction, step):
                    copy.wait_send()
    for direction, piece in lanes:
        for hop in range(1, hops(direction, piece) + 1):
            reduce_copy(direction, piece, hop).wait_send()


def body(
    cotangent, gates, routes, slots, saved_hidden, left_wide, left_narrow, right_wide, right_narrow
):
    ring, experts = lax.axis_size("dp"), lax.axis_size("expert")
    capacity, width = saved_hidden.shape[3:]
    z = Sizes(
        ring, experts, capacity, width, left_wide.shape[1], left_narrow.shape[1],
        cotangent.shape[0], gates.shape[1],
    )
    vmem = pl.BlockSpec(memory_space=pltpu.VMEM)
    ow, on = pl.pallas_call(
        functools.partial(kernel, z),
        out_shape=(
            jax.ShapeDtypeStruct((z.cw, 1, z.width), F32),
            jax.ShapeDtypeStruct((z.cn, 1, z.width), F32),
        ),
        in_specs=[vmem] * 4 + [pl.BlockSpec(memory_space=pl.ANY)] + [vmem] * 4,
        out_specs=(vmem, vmem),
        scratch_shapes=[
            pltpu.VMEM((z.side, z.side, 2, capacity, width), BF),
            pltpu.VMEM((2, z.side, z.side, 2, z.rows, z.tokens), BF),
            pltpu.VMEM((z.depth, z.sources * z.tokens), BF),
            pltpu.VMEM((z.part, 2 * z.depth), BF),
            pltpu.VMEM((width, width), F32),
            pltpu.VMEM((width, width), BF),
            pltpu.VMEM((ring, z.cwp, z.packed), BF),
            pltpu.VMEM((ring, z.cnp, z.narrow), BF),
            pltpu.VMEM((ring, z.cwp, z.packed), BF),
            pltpu.VMEM((ring, z.cnp, z.narrow), BF),
            pltpu.VMEM((z.tail, z.folded), BF),
            pltpu.VMEM((ring, z.seg, z.kept), BF),
            pltpu.VMEM((2, z.half, z.seg, z.kept), BF),
            pltpu.VMEM((z.wide, z.wide), BF),
            pltpu.VMEM((z.narrow, z.narrow), BF),
            pltpu.SemaphoreType.DMA((experts,)),
            pltpu.SemaphoreType.DMA((2, 2, 2)),
            pltpu.SemaphoreType.DMA((2, 2, 2)),
            pltpu.SemaphoreType.DMA((2, 2, z.side, 2)),
            pltpu.SemaphoreType.DMA((2, 2, z.side, 2)),
            pltpu.SemaphoreType.DMA((2, z.side, z.side)),
            pltpu.SemaphoreType.DMA((2, z.side, z.side)),
            pltpu.SemaphoreType.DMA((2, 2, z.half, 1)),
            pltpu.SemaphoreType.DMA((2, 2, z.half, 1)),
            pltpu.SemaphoreType.DMA((2, 2, z.half)),
            pltpu.SemaphoreType.DMA((2, 2, z.half)),
        ],
        compiler_params=pltpu.CompilerParams(
            collective_id=0, has_side_effects=True, vmem_limit_bytes=60 * 1024 * 1024
        ),
        cost_estimate=pl.CostEstimate(flops=10_000_000_000, bytes_accessed=8_000_000, transcendentals=0),
    )(
        cotangent.T, gates.T, routes.T, slots.T,
        saved_hidden.reshape(experts, capacity, width),
        left_wide[0].T, left_narrow[0].T, right_wide[0].T, right_narrow[0].T,
    )
    return jnp.transpose(ow, (1, 2, 0)), jnp.transpose(on, (1, 2, 0))


def solution(mesh):
    return jax.shard_map(
        body,
        mesh=mesh,
        in_specs=(
            P(("dp", "expert"), None),
            P(("dp", "expert"), None),
            P(("dp", "expert"), None),
            P(("dp", "expert"), None),
            P("dp", "expert", None, None, None),
            P("expert", None, "dp"),
            P("expert", None, "dp"),
            P("expert", None, "dp"),
            P("expert", None, "dp"),
        ),
        out_specs=(P("expert", None, "dp"), P("expert", None, "dp")),
        check_vma=False,
    )
```
